128 devices in a mesh: row: 16 (over z, y), col: 8 (over x, core).
Axes of the slice: x: 4, y: 4, z: 4, core: 2. Of those that a mesh axis runs over, the one named last changes fastest.
Arguments:
- queries: bfloat16 [4096, 480], P('row'), may hold values from -64 to 64
- keys: bfloat16 [4096, 960], P(('col', 'row')), may hold values from -32 to 32
- frame_table: float32 [12, 4096], replicated, may hold values from -6 to 6, as said below
- frame_index: int32 [4096], replicated, may hold values from 0 to 4095, each once
- pair_list: int32 [16, 8, 2], P('row', 'col'), may hold values from 0 to 8, as said below
- pair: bfloat16 [16, 8, 2, 128, 128, 128], P('row', 'col'), may hold values from -6 to 6
- pair_weight: bfloat16 [128, 12], replicated, may hold values from -0.5 to 0.5
- point_weight: float32 [12], replicated, may hold values from -2.5 to 1
- out_weight: bfloat16 [2016, 384], replicated, may hold values from -0.125 to 0.125
- cotangent: bfloat16 [4096, 384], P('row'), may hold values from -6 to 6
Outputs:
- update: bfloat16 [4096, 384], P(('row', 'col'))
- grad_queries: bfloat16 [4096, 480], P(('row', 'col'))
- grad_keys: bfloat16 [4096, 960], P(('col', 'row'))
- grad_pair: bfloat16 [16, 8, 2, 128, 128, 128], P('row', 'col')
The draws below stay inside these ranges and needn't reach their ends.
Inputs may be any that keep to these rules, and one draw needn't show every extreme that they name: `pair_list`: A value below 8 names a local pair (query block value // 4 of the row index, key block value % 4 of the col index); 8 marks an empty slot. The slots of one device name distinct pairs, and every query block's own block is listed as a key block. Listed pairs lie near the diagonal, with a few far ones. `frame_table`: rotation rows form orthonormal matrices.
All inputs are finite; a program needn't handle non-finite values.
Results may differ from the reference program's by a relative error of at most 0.03.
Values may be sent and summed in bfloat16 or wider, within the bound.
No kernel may reach another device: no remote copies, remote signals or barrier semaphores. Data moves between devices by JAX's collectives and lax.ppermute only.
A program may use at most 128 MiB of HBM per device.

```python
import math
import jax
import jax.numpy as jnp
from jax import lax

H = 12
C = 16
P_SIZE = 8
PV = 8
PW = 128
SW = 384
BLK = 128
QB_DEV = 2
KB_DEV = 4
CAP = 2
NRES = 4096
QR = 256
QF = 480
KF = 960
OF = 2016
N_ROW = 16
N_COL = 8


def key_scalars(key):
    base = jnp.clip(jax.random.normal(jax.random.fold_in(key, 11), (NRES, H * C), jnp.float32), -4.0, 4.0)
    return base


def draw_keys(key, part):
    scalars = key_scalars(key)
    shape = (NRES, H * C + 3 * H * P_SIZE + 3 * H * PV)
    others = jnp.clip(jax.random.normal(jax.random.fold_in(key, 12), shape, jnp.float32), -4.0, 4.0)
    return jnp.concatenate([scalars, others], axis=1).astype(jnp.bfloat16)


def draw_queries(key, part):
    own_scalars = jnp.clip(jax.random.normal(jax.random.fold_in(key, 13), (NRES, H * C), jnp.float32), -4.0, 4.0)
    points = jnp.clip(jax.random.normal(jax.random.fold_in(key, 14), (NRES, 3 * H * P_SIZE), jnp.float32), -4.0, 4.0)
    return jnp.concatenate([own_scalars, points], axis=1).astype(jnp.bfloat16)


def draw_frame_table(key, part):
    quats = jax.random.normal(jax.random.fold_in(key, 21), (4, NRES), jnp.float32)
    quats = quats / jnp.sqrt(jnp.sum(quats * quats, axis=0, keepdims=True) + 1e-12)
    qw, qx, qy, qz = (quats[0], quats[1], quats[2], quats[3])
    rows = [1.0 - 2.0 * (qy * qy + qz * qz), 2.0 * (qx * qy - qw * qz), 2.0 * (qx * qz + qw * qy), 2.0 * (qx * qy + qw * qz), 1.0 - 2.0 * (qx * qx + qz * qz), 2.0 * (qy * qz - qw * qx), 2.0 * (qx * qz - qw * qy), 2.0 * (qy * qz + qw * qx), 1.0 - 2.0 * (qx * qx + qy * qy)]
    shifts = jnp.clip(jax.random.normal(jax.random.fold_in(key, 22), (3, NRES), jnp.float32), -3.0, 3.0)
    return jnp.concatenate([jnp.stack(rows, axis=0), shifts], axis=0).astype(jnp.float32)


def draw_pair_list(key, part):
    codes_total = QB_DEV * KB_DEV
    row_ids = jnp.arange(N_ROW, dtype=jnp.int32)[:, None]
    col_ids = jnp.arange(N_COL, dtype=jnp.int32)[None, :]
    diagonal_col = row_ids * QB_DEV // KB_DEV
    distance = jnp.abs(col_ids - diagonal_col)
    near_count = jax.random.randint(jax.random.fold_in(key, 31), (N_ROW, N_COL), 0, CAP + 1)
    far_pick = jax.random.randint(jax.random.fold_in(key, 32), (N_ROW, N_COL), 0, 4)
    far_count = jnp.where((far_pick == 0) & (row_ids % 2 == 1), 1, 0)
    slot_total = jnp.where(distance == 0, CAP, jnp.where(distance == 1, near_count, far_count))
    scores = jax.random.randint(jax.random.fold_in(key, 33), (N_ROW, N_COL, codes_total), 0, 1 << 20) * codes_total + jnp.arange(codes_total, dtype=jnp.int32)
    order = jnp.argsort(-scores, axis=-1)[..., :CAP].astype(jnp.int32)
    slot_ids = jnp.arange(CAP, dtype=jnp.int32)[None, None, :]
    diagonal_code = slot_ids * KB_DEV + (row_ids[..., None] * QB_DEV + slot_ids - diagonal_col[..., None] * KB_DEV)
    listed = jnp.where(slot_ids < slot_total[..., None], order, codes_total)
    return jnp.where((distance == 0)[..., None], diagonal_code, listed).astype(jnp.int32)


def steps_of(stream_key, dims, pieces, smallest, largest):
    gain = 1.0
    for axis_at, parts in pieces:
        steps = jax.random.uniform(jax.random.fold_in(jax.random.fold_in(stream_key, 6), axis_at), (parts,), jnp.float32, smallest / len(pieces), largest / len(pieces))
        gain = gain * jnp.repeat(jnp.exp(steps), dims[axis_at] // parts).reshape((-1,) + (1,) * (len(dims) - 1 - axis_at))
    return gain


def scatter_about(key, extent, scale, limit, cuts=(), kind=jnp.bfloat16):
    level = steps_of(key, extent, cuts, -0.22, 0.18) if cuts else 1.0
    drawn = jax.random.normal(key, extent, jnp.float32) * scale * level
    return jnp.minimum(jnp.maximum(drawn, -limit), limit).astype(kind)


def setup_inputs(seed: int = 0) -> dict:
    streams_of = jax.random.split(jax.random.key(seed), 11)
    return {
        "queries": draw_queries(jax.random.fold_in(streams_of[10], 71), 0),
        "keys": draw_keys(jax.random.fold_in(streams_of[10], 71), 0),
        "frame_table": draw_frame_table(jax.random.fold_in(streams_of[10], 71), 0),
        "frame_index": jax.random.permutation(streams_of[3], NRES).astype(jnp.int32),
        "pair_list": draw_pair_list(jax.random.fold_in(streams_of[10], 71), 0),
        "pair": scatter_about(streams_of[5], (N_ROW, N_COL, CAP, BLK, BLK, PW), 1.0, 6.0, ((0, 16), (1, 8))),
        "pair_weight": scatter_about(streams_of[6], (PW, H), PW ** -0.5, 0.5),
        "point_weight": jnp.clip(jax.random.uniform(streams_of[7], (H,), jnp.float32, -2.5, 1.0), -2.5, 1.0),
        "out_weight": scatter_about(streams_of[8], (OF, SW), OF ** -0.5, 0.125),
        "cotangent": scatter_about(streams_of[9], (NRES, SW), 1.0, 6.0, ((0, 16),)),
    }


NEG_FILL = -1e+30
HIGH = lax.Precision.HIGHEST

def frame_parts(columns):
    rotation = columns[:9].T.reshape(-1, 3, 3)
    return (rotation, columns[9:].T)

def to_global(local, rotation, offset):
    return jnp.einsum('nab,nbk->nak', rotation, local, precision=HIGH) + offset[:, :, None]

def to_local(vector, rotation):
    return jnp.einsum('nab,nak->nbk', rotation, vector, precision=HIGH)

def add_rows(total, part, start):
    older = lax.dynamic_slice_in_dim(total, start, part.shape[0], 0)
    return lax.dynamic_update_slice_in_dim(total, older + part, start, 0)

def block_of(array, first):
    return lax.dynamic_slice_in_dim(array, first, BLK, 0)

def as_float(array):
    return array.astype(jnp.float32)

def rounded_float(array):
    return lax.optimization_barrier(array.astype(jnp.bfloat16)).astype(jnp.float32)

def reference(queries, keys, frame_table, frame_index, pair_list, pair, pair_weight, point_weight, out_weight, cotangent):
    width_scalar = H * C
    width_point = 3 * H * P_SIZE
    width_value = 3 * H * PV
    width_pair = H * PW
    scale_scalar = 1.0 / math.sqrt(C)
    scale_point = math.sqrt(2.0 / (9.0 * P_SIZE))
    scale_logit = math.sqrt(1.0 / 3.0)
    empty_code = QB_DEV * KB_DEV
    head_gamma = jax.nn.softplus(point_weight)
    rotation, offset = frame_parts(jnp.take(frame_table, frame_index, axis=1))
    query_scalar = queries[:, :width_scalar].reshape(NRES, H, C)
    query_point = to_global(as_float(queries[:, width_scalar:]).reshape(NRES, 3, H * P_SIZE), rotation, offset).astype(jnp.bfloat16).reshape(NRES, 3, H, P_SIZE)
    key_scalar = keys[:, :width_scalar].reshape(NRES, H, C)
    value_scalar = keys[:, width_scalar:2 * width_scalar].reshape(NRES, H, C)
    point_start = 2 * width_scalar
    key_point = to_global(as_float(keys[:, point_start:point_start + width_point]).reshape(NRES, 3, H * P_SIZE), rotation, offset).astype(jnp.bfloat16).reshape(NRES, 3, H, P_SIZE)
    value_point = to_global(as_float(keys[:, point_start + width_point:]).reshape(NRES, 3, H * PV), rotation, offset).astype(jnp.bfloat16).reshape(NRES, 3, H, PV)
    grad_feat = jnp.dot(cotangent, out_weight.T, preferred_element_type=jnp.float32).astype(jnp.bfloat16)
    grad_scalar = grad_feat[:, :width_scalar].reshape(NRES, H, C)
    grad_value = jnp.einsum('nab,nbk->nak', rotation, as_float(grad_feat[:, width_scalar:width_scalar + width_value]).reshape(NRES, 3, H * PV), precision=HIGH).astype(jnp.bfloat16).reshape(NRES, 3, H, PV)
    grad_pairout = grad_feat[:, width_scalar + width_value:].reshape(NRES, H, PW)
    slot_count = N_COL * CAP
    slot_column = jnp.repeat(jnp.arange(N_COL, dtype=jnp.int32), CAP)
    gamma_point = head_gamma[None, None, :, None]

    def one_row(key_total, row_index):
        row_base = row_index * QR
        codes = pair_list[row_index].reshape(slot_count).astype(jnp.int32)
        tiles = pair[row_index].reshape(slot_count, BLK, BLK, PW)
        listed = codes < empty_code
        safe_code = jnp.where(listed, codes, 0)
        query_start = (safe_code // KB_DEV * BLK).astype(jnp.int32)
        key_start = ((slot_column * KB_DEV + safe_code % KB_DEV) * BLK).astype(jnp.int32)
        rot_row = lax.dynamic_slice_in_dim(rotation, row_base, QR, 0)
        off_row = lax.dynamic_slice_in_dim(offset, row_base, QR, 0)
        grad_s_row = lax.dynamic_slice_in_dim(grad_scalar, row_base, QR, 0)
        grad_v_row = lax.dynamic_slice_in_dim(grad_value, row_base, QR, 0)
        grad_z_row = lax.dynamic_slice_in_dim(grad_pairout, row_base, QR, 0)

        def pieces_of(number):
            query_row = row_base + query_start[number]
            key_row = key_start[number]
            return (block_of(query_scalar, query_row), block_of(query_point, query_row), block_of(key_scalar, key_row), block_of(value_scalar, key_row), block_of(key_point, key_row), block_of(value_point, key_row), tiles[number])

        def logit_of(number):
            query_block, query_spot, key_block, value_block, key_spot, value_spot, pair_tile = pieces_of(number)
            scalar_term = jnp.einsum('ihc,jhc->hij', as_float(query_block), as_float(key_block), precision=HIGH)
            bias_term = jnp.einsum('ijc,ch->hij', as_float(pair_tile), as_float(pair_weight), precision=HIGH)
            spread = as_float(query_spot)[:, None] - as_float(key_spot)[None, :]
            distance = lax.optimization_barrier(jnp.sum(spread * spread, axis=(2, 4))).transpose(2, 0, 1)
            logit_block = scale_logit * (scale_scalar * scalar_term + bias_term - 0.5 * scale_point * head_gamma[:, None, None] * distance)
            return jnp.where(listed[number], logit_block, NEG_FILL)
        logits = lax.map(logit_of, jnp.arange(slot_count, dtype=jnp.int32))

        def max_step(number, running):
            slot_max = lax.optimization_barrier(jnp.max(logits[number], axis=2)).T
            start = query_start[number]
            older = lax.dynamic_slice_in_dim(running, start, BLK, 0)
            return lax.dynamic_update_slice_in_dim(running, jnp.maximum(older, slot_max), start, 0)
        row_max = lax.fori_loop(0, slot_count, max_step, jnp.full((QR, H), NEG_FILL, jnp.float32))

        def sum_step(number, totals):
            query_block, query_spot, key_block, value_block, key_spot, value_spot, pair_tile = pieces_of(number)
            start = query_start[number]
            max_block = lax.dynamic_slice_in_dim(row_max, start, BLK, 0)
            weights = jnp.where(listed[number], jnp.exp(logits[number] - max_block.T[:, :, None]), 0.0)
            rounded = rounded_float(weights)
            part_total = lax.optimization_barrier(jnp.sum(weights, axis=2)).T
            part_scalar = jnp.einsum('hij,jhc->ihc', rounded, as_float(value_block), precision=HIGH).reshape(BLK, width_scalar)
            part_value = jnp.einsum('hij,jdhp->idhp', rounded, as_float(value_spot), precision=HIGH).reshape(BLK, width_value)
            part_pair = jnp.einsum('hij,ijc->ihc', rounded, as_float(pair_tile), precision=HIGH).reshape(BLK, width_pair)
            return (add_rows(totals[0], part_total, start), add_rows(totals[1], part_scalar, start), add_rows(totals[2], part_value, start), add_rows(totals[3], part_pair, start))
        start_totals = (jnp.zeros((QR, H), jnp.float32), jnp.zeros((QR, width_scalar), jnp.float32), jnp.zeros((QR, width_value), jnp.float32), jnp.zeros((QR, width_pair), jnp.float32))
        totals = lax.fori_loop(0, slot_count, sum_step, start_totals)
        denominator = totals[0]
        out_scalar = totals[1].reshape(QR, H, C) / denominator[:, :, None]
        out_value = totals[2].reshape(QR, 3, H, PV) / denominator[:, None, :, None]
        out_pair = totals[3].reshape(QR, H, PW) / denominator[:, :, None]
        local_value = to_local(out_value.reshape(QR, 3, H * PV) - off_row[:, :, None], rot_row)
        feat = jnp.concatenate([out_scalar.reshape(QR, width_scalar), local_value.reshape(QR, width_value), out_pair.reshape(QR, width_pair)], axis=1).astype(jnp.bfloat16)
        update_row = jnp.dot(feat, out_weight, preferred_element_type=jnp.float32).astype(jnp.bfloat16)
        delta = lax.optimization_barrier(jnp.sum(as_float(grad_s_row) * out_scalar, axis=2)) + lax.optimization_barrier(jnp.sum(as_float(grad_v_row) * out_value, axis=(1, 3))) + lax.optimization_barrier(jnp.sum(as_float(grad_z_row) * out_pair, axis=2))
        log_total = row_max + jnp.log(denominator)

        def back_step(number, carry):
            query_total, key_inner, tile_grads = carry
            query_block, query_spot, key_block, value_block, key_spot, value_spot, pair_tile = pieces_of(number)
            start = query_start[number]
            lse_block = lax.dynamic_slice_in_dim(log_total, start, BLK, 0)
            delta_block = lax.dynamic_slice_in_dim(delta, start, BLK, 0)
            grad_s_block = as_float(lax.dynamic_slice_in_dim(grad_s_row, start, BLK, 0))
            grad_v_block = as_float(lax.dynamic_slice_in_dim(grad_v_row, start, BLK, 0))
            grad_z_block = as_float(lax.dynamic_slice_in_dim(grad_z_row, start, BLK, 0))
            weights = jnp.where(listed[number], jnp.exp(logits[number] - lse_block.T[:, :, None]), 0.0)
            rounded = rounded_float(weights)
            touch = jnp.einsum('ihc,jhc->hij', grad_s_block, as_float(value_block), precision=HIGH)
            touch = touch + jnp.einsum('idhp,jdhp->hij', grad_v_block, as_float(value_spot), precision=HIGH)
            touch = touch + jnp.einsum('ihc,ijc->hij', grad_z_block, as_float(pair_tile), precision=HIGH)
            score_grad = rounded_float(scale_logit * weights * (touch - delta_block.T[:, :, None]))
            tile_grad = (jnp.einsum('hij,ihc->ijc', rounded, grad_z_block, precision=HIGH) + jnp.einsum('hij,ch->ijc', score_grad, as_float(pair_weight), precision=HIGH)).astype(jnp.bfloat16)
            row_sum = lax.optimization_barrier(jnp.sum(score_grad, axis=2)).T
            col_sum = lax.optimization_barrier(jnp.sum(score_grad, axis=1)).T
            grad_q_scalar = scale_scalar * jnp.einsum('hij,jhc->ihc', score_grad, as_float(key_block), precision=HIGH)
            grad_q_point = -scale_point * gamma_point * (row_sum[:, None, :, None] * as_float(query_spot) - jnp.einsum('hij,jdhp->idhp', score_grad, as_float(key_spot), precision=HIGH))
            grad_k_scalar = scale_scalar * jnp.einsum('hij,ihc->jhc', score_grad, as_float(query_block), precision=HIGH)
            grad_k_point = -scale_point * gamma_point * (col_sum[:, None, :, None] * as_float(key_spot) - jnp.einsum('hij,idhp->jdhp', score_grad, as_float(query_spot), precision=HIGH))
            grad_v_scalar = jnp.einsum('hij,ihc->jhc', rounded, grad_s_block, precision=HIGH)
            grad_v_point = jnp.einsum('hij,idhp->jdhp', rounded, grad_v_block, precision=HIGH)
            query_part = jnp.concatenate([grad_q_scalar.reshape(BLK, width_scalar), grad_q_point.reshape(BLK, width_point)], axis=1)
            key_part = jnp.concatenate([grad_k_scalar.reshape(BLK, width_scalar), grad_v_scalar.reshape(BLK, width_scalar), grad_k_point.reshape(BLK, width_point), grad_v_point.reshape(BLK, width_value)], axis=1)
            return (add_rows(query_total, query_part, start), add_rows(key_inner, key_part, key_start[number]), tile_grads.at[number].set(tile_grad))
        start_back = (jnp.zeros((QR, QF), jnp.float32), key_total, jnp.zeros((slot_count, BLK, BLK, PW), jnp.bfloat16))
        query_total, key_total, tile_grads = lax.fori_loop(0, slot_count, back_step, start_back)
        query_local = to_local(query_total[:, width_scalar:].reshape(QR, 3, H * P_SIZE), rot_row)
        grad_query_row = jnp.concatenate([query_total[:, :width_scalar], query_local.reshape(QR, width_point)], axis=1).astype(jnp.bfloat16)
        return (key_total, (update_row, grad_query_row, tile_grads))
    key_total, stacked = lax.scan(one_row, jnp.zeros((NRES, KF), jnp.float32), jnp.arange(N_ROW, dtype=jnp.int32))
    update = stacked[0].reshape(NRES, SW)
    grad_queries = stacked[1].reshape(NRES, QF)
    grad_pair = stacked[2].reshape(N_ROW, N_COL, CAP, BLK, BLK, PW)
    key_local = to_local(key_total[:, point_start:point_start + width_point].reshape(NRES, 3, H * P_SIZE), rotation)
    value_local = to_local(key_total[:, point_start + width_point:].reshape(NRES, 3, H * PV), rotation)
    grad_keys = jnp.concatenate([key_total[:, :point_start], key_local.reshape(NRES, width_point), value_local.reshape(NRES, width_value)], axis=1).astype(jnp.bfloat16)
    return (update, grad_queries, grad_keys, grad_pair)
```

```python
import functools
import math

import jax
import jax.numpy as jnp
import numpy as np
from jax import lax
from jax.experimental import pallas as pl
from jax.experimental.pallas import tpu as pltpu
from jax.sharding import PartitionSpec as P

H = 12
C = 16
PV = 8
PW = 128
BLK = 128
SW = 384
QR = 256
KR = 512
NRES = 4096
KEYB = 4
CAP = 2
F = 480
WS = 192
WP = 288
HJ = H * BLK
N_ROW = 16
N_COL = 8
OWN = 32
IB = 32
EMPTY = 8
NEG = -1e30
SC = 1.0 / math.sqrt(C)
WC = math.sqrt(2.0 / 72.0)
WL = math.sqrt(1.0 / 3.0)
F32 = jnp.float32
BF16 = jnp.bfloat16
VMEM_LIMIT = 56 * 1024 * 1024

NN = (((1,), (0,)), ((), ()))
NT = (((1,), (1,)), ((), ()))
TN = (((0,), (0,)), ((), ()))


def head_rows():
    f = np.arange(F)
    head = np.where(f < WS, f // C, ((f - WS) % (H * PV)) // PV)
    return (head[None, :] == np.arange(16)[:, None]).astype(np.float32)


def dot(a, b, dims=NN):
    return lax.dot_general(a, b, dims, preferred_element_type=F32)


def split3(x):
    hi = x.astype(BF16)
    rest = x - hi.astype(F32)
    mid = rest.astype(BF16)
    lo = (rest - mid.astype(F32)).astype(BF16)
    return hi, mid, lo


def rotate(x, frame, shift):
    parts = [x[:, 96 * b : 96 * b + 96] for b in range(3)]
    out = []
    for a in range(3):
        y = sum(frame[:, 3 * a + b : 3 * a + b + 1] * parts[b] for b in range(3))
        if shift:
            y = y + frame[:, 9 + a : 10 + a]
        out.append(y)
    return jnp.concatenate(out, axis=1)


def rotate_back(x, frame, shift):
    parts = [x[:, 96 * a : 96 * a + 96] for a in range(3)]
    if shift:
        parts = [parts[a] - frame[:, 9 + a : 10 + a] for a in range(3)]
    out = []
    for b in range(3):
        out.append(sum(frame[:, 3 * a + b : 3 * a + b + 1] * parts[a] for a in range(3)))
    return jnp.concatenate(out, axis=1)


def slot_of(codes_ref, s):
    code = codes_ref[s]
    listed = code < EMPTY
    safe = jnp.where(listed, code, 0)
    return listed, safe // KEYB, safe % KEYB


def rows_of(block):
    return pl.ds(pl.multiple_of(block * BLK, BLK), BLK)


def prep_kernel(pos_ref, q_ref, table_ref, index_ref, cot_ref, ow_ref, pwt_ref,
                qf_ref, df_ref, dzp_ref, frame_ref):
    row = pos_ref[0]
    col = pos_ref[1]
    ids = jnp.concatenate(
        [
            index_ref[:, pl.ds(pl.multiple_of(row * QR, QR), QR)],
            index_ref[:, pl.ds(pl.multiple_of(col * KR, KR), KR)],
        ],
        axis=1,
    )
    table = jnp.concatenate([table_ref[...], jnp.zeros((4, NRES), F32)], axis=0)
    table = jnp.concatenate(split3(table), axis=0)
    found = jnp.zeros((48, QR + KR), F32)
    step = 512
    for first in range(0, NRES, step):
        at = lax.broadcasted_iota(jnp.int32, (step, QR + KR), 0) + first
        hot = jnp.where(at == ids, 1.0, 0.0).astype(BF16)
        found = found + dot(table[:, first : first + step], hot)
    frame_t = found[0:16] + found[16:32] + found[32:48]
    frame_ref[...] = frame_t
    frame = jnp.transpose(frame_t[:, :QR])
    q = q_ref[...]
    gq = rotate(q[:, WS:].astype(F32), frame, True).astype(BF16)
    qf_ref[...] = jnp.concatenate([q[:, :WS], gq], axis=1)
    cot = cot_ref[...]
    head = dot(cot, ow_ref[0:F], NT).astype(BF16)
    gd = rotate(head[:, WS:].astype(F32), frame, False).astype(BF16)
    df_ref[...] = jnp.concatenate([head[:, :WS], gd], axis=1)
    tail = dot(cot, ow_ref[F:], NT).astype(BF16).astype(F32)
    pwt = pwt_ref[...].astype(F32)
    for h in range(H):
        dzp_ref[:, h, :] = jnp.broadcast_to(pwt[h : h + 1], (QR, PW))
        dzp_ref[:, H + h, :] = tail[:, h * PW : (h + 1) * PW]


def pair_in_kernel(codes_ref, pair_ref, dzp_ref, out_ref):
    _, qb, _ = slot_of(codes_ref, pl.program_id(0))
    first = qb * BLK + pl.program_id(1) * IB
    for i in range(IB):
        lhs = dzp_ref[first + i].astype(BF16)
        out_ref[0, :, i, :] = dot(lhs, pair_ref[0, i], NT)


def logit_kernel(codes_ref, keys_ref, frame_ref, qf_ref, df_ref, bz_ref, e_ref, gam_ref,
                 logit_ref, da_ref, kf_ref, vf_ref, stat_ref):
    e = e_ref[...]
    lane = lax.broadcasted_iota(jnp.int32, (BLK, BLK), 1)
    stats = []
    for s in range(CAP):
        listed, qb, kb = slot_of(codes_ref, s)
        raw = keys_ref[rows_of(kb), :]
        frame = jnp.transpose(frame_ref[:, pl.ds(pl.multiple_of(QR + kb * BLK, BLK), BLK)])
        spot = raw[:, 2 * WS :].astype(F32)
        gk = rotate(spot[:, :WP], frame, True).astype(BF16)
        gv = rotate(spot[:, WP:], frame, True).astype(BF16)
        kf = jnp.concatenate([raw[:, :WS], gk], axis=1)
        vf = jnp.concatenate([raw[:, WS : 2 * WS], gv], axis=1)
        kf_ref[s] = kf
        vf_ref[s] = vf
        qf = qf_ref[rows_of(qb), :]
        df = df_ref[rows_of(qb), :]
        qp = qf[:, WS:]
        ep = e[:, WS:]
        qsq = jnp.square(qp.astype(F32))
        ksq = jnp.square(gk.astype(F32))
        qhi = qsq.astype(BF16)
        qlo = (qsq - qhi.astype(F32)).astype(BF16)
        khi = ksq.astype(BF16)
        klo = (ksq - khi.astype(F32)).astype(BF16)
        qn = dot(qhi, ep, NT) + dot(qlo, ep, NT)
        kn = dot(ep, khi, NT) + dot(ep, klo, NT)
        held = jnp.zeros((BLK, BLK), F32)
        for h in range(H):
            eh = e[h : h + 1]
            kh = kf * eh
            vh = vf * eh
            scal = dot(qf[:, :WS], kh[:, :WS], NT)
            cross = dot(qp, kh[:, WS:], NT)
            dist = qn[:, h : h + 1] + kn[h : h + 1, :] - 2.0 * cross
            logit = (WL * SC) * scal + WL * bz_ref[s, h] - (0.5 * WL * WC) * gam_ref[h : h + 1] * dist
            da = bz_ref[s, H + h] + dot(df, vh, NT)
            logit_ref[s, h] = logit
            da_ref[s, h] = da
            top = jnp.max(logit, axis=1, keepdims=True)
            p = jnp.exp(logit - top)
            total = jnp.sum(p, axis=1, keepdims=True)
            mean = jnp.sum(p * da, axis=1, keepdims=True) / total
            held = jnp.where(lane == h, top + jnp.log(total), held)
            held = jnp.where(lane == 16 + h, mean, held)
        stats.append((listed, qb, jnp.transpose(held)))
    for b in range(2):
        lse = []
        for listed, qb, held in stats:
            lse.append(jnp.where(jnp.logical_and(listed, qb == b), held[0:16], NEG))
        top = jnp.maximum(lse[0], lse[1])
        w0 = jnp.exp(lse[0] - top)
        w1 = jnp.exp(lse[1] - top)
        total = w0 + w1
        stat_ref[0:16, b * BLK : (b + 1) * BLK] = top + jnp.log(total)
        stat_ref[16:32, b * BLK : (b + 1) * BLK] = (
            w0 * stats[0][2][16:32] + w1 * stats[1][2][16:32]
        ) / total


def out_kernel(codes_ref, pair_ref, logit_ref, vf_ref, stat_ref, e_ref, o_ref, p_ref, nz_ref, cat_ref, bd_ref):
    s = pl.program_id(0)
    step = pl.program_id(1)
    listed, qb, _ = slot_of(codes_ref, s)

    @pl.when(jnp.logical_and(s == 0, step == 0))
    def _():
        o_ref[...] = jnp.zeros_like(o_ref)

    @pl.when(step == 0)
    def _():
        lse = jnp.transpose(stat_ref[0:16, rows_of(qb)])
        lse = jnp.where(listed, lse, -NEG)
        vf = vf_ref[0]
        for h in range(H):
            p = jnp.exp(logit_ref[0, h] - lse[:, h : h + 1])
            p_ref[h] = p
            cat_ref[:, h * BLK : (h + 1) * BLK] = p.astype(BF16)
            bd_ref[h * BLK : (h + 1) * BLK, :] = vf * e_ref[h : h + 1, :]
        o_ref[rows_of(qb), 0:F] += dot(cat_ref[...], bd_ref[...])

    first = step * IB
    for i in range(IB):
        w = p_ref[:, first + i, :].astype(BF16)
        nz_ref[:, first + i, :] = dot(w, pair_ref[0, i])

    @pl.when(step == pl.num_programs(1) - 1)
    def _():
        for h in range(H):
            o_ref[rows_of(qb), 512 + h * PW : 512 + (h + 1) * PW] += nz_ref[h]


def back_kernel(codes_ref, all_ref, stat_ref, logit_ref, da_ref, kf_ref, vf_ref, qf_ref, df_ref, e_ref, gam_ref,
                o_ref, ga_ref, msg_ref, kg_ref, kg_acc, gcat, gstk, astk, kbd, qbd, dbd, ebd, dq_acc):
    top = all_ref[0, 0:16]
    for d in range(1, N_COL):
        top = jnp.maximum(top, all_ref[d, 0:16])
    total = jnp.zeros((16, QR), F32)
    mean = jnp.zeros((16, QR), F32)
    for d in range(N_COL):
        w = jnp.exp(all_ref[d, 0:16] - top)
        total = total + w
        mean = mean + w * all_ref[d, 16:32]
    lse = top + jnp.log(total)
    delta = mean / total
    alpha = jnp.transpose(jnp.exp(stat_ref[0:16] - lse))
    both = jnp.transpose(jnp.concatenate([lse, delta], axis=0))
    e = e_ref[...]
    ahi = alpha.astype(BF16)
    alo = (alpha - ahi.astype(F32)).astype(BF16)
    spread = dot(ahi, e) + dot(alo, e)
    msg_ref[:, 0:F] = (o_ref[:, 0:F] * spread).astype(BF16)
    for h in range(H):
        msg_ref[:, 512 + h * PW : 512 + (h + 1) * PW] = (
            o_ref[:, 512 + h * PW : 512 + (h + 1) * PW] * alpha[:, h : h + 1]
        ).astype(BF16)
    gam_f = jnp.sum(e.astype(F32) * gam_ref[:, 0:1], axis=0, keepdims=True)
    point = lax.broadcasted_iota(jnp.int32, (1, F), 1) >= WS
    fa = jnp.where(point, WC * gam_f, SC)
    fb = jnp.where(point, -WC * gam_f, 0.0)
    kg_acc[...] = jnp.zeros_like(kg_acc)
    dq_acc[...] = jnp.zeros_like(dq_acc)
    for h in range(H):
        ebd[h * BLK : (h + 1) * BLK, :] = jnp.broadcast_to(e[h : h + 1], (BLK, F))
    for s in range(CAP):
        listed, qb, kb = slot_of(codes_ref, s)
        stat_ref_b = jnp.where(qb == 0, both[0:BLK], both[BLK:])
        kf = kf_ref[s]
        vf = vf_ref[s]
        qf = qf_ref[rows_of(qb), :]
        df = df_ref[rows_of(qb), :]
        for h in range(H):
            block = slice(h * BLK, (h + 1) * BLK)
            a = jnp.exp(logit_ref[s, h] - jnp.where(listed, stat_ref_b[:, h : h + 1], -NEG))
            g = WL * a * (da_ref[s, h] - stat_ref_b[:, 16 + h : 17 + h])
            gr = g.astype(BF16)
            ar = a.astype(BF16)
            ga_ref[s, h] = g
            ga_ref[s, H + h] = a
            gcat[:, block] = gr
            gstk[block, :] = gr
            astk[block, :] = ar
            eh = e[h : h + 1]
            kbd[block, :] = kf * eh
            qbd[block, :] = qf * eh
            dbd[block, :] = df * eh
        dq_raw = dot(gcat[...], kbd[...])
        row_sum = dot(gcat[...], ebd[...])
        dq_acc[rows_of(qb), :] += fa * dq_raw + fb * row_sum * qf.astype(F32)
        dk_raw = dot(gstk[...], qbd[...], TN)
        col_sum = dot(gstk[...], ebd[...], TN)
        kg_acc[rows_of(kb), 0:F] += fa * dk_raw + fb * col_sum * kf.astype(F32)
        kg_acc[rows_of(kb), 512 : 512 + F] += dot(astk[...], dbd[...], TN)
    kg_ref[...] = kg_acc[...].astype(BF16)
    msg_ref[:, 2048 : 2048 + F] = dq_acc[...].astype(BF16)


def pair_out_kernel(codes_ref, ga_ref, dzp_ref, out_ref):
    _, qb, _ = slot_of(codes_ref, pl.program_id(0))
    first = qb * BLK + pl.program_id(1) * IB
    for i in range(IB):
        lhs = ga_ref[0, :, i, :].astype(BF16)
        rhs = dzp_ref[first + i].astype(BF16)
        out_ref[0, i] = dot(lhs, rhs, TN).astype(BF16)


def final_kernel(pos_ref, kg_ref, msg_ref, frame_ref, ow_ref, up_ref, gq_ref, gk_ref):
    row = pos_ref[0]
    col = pos_ref[1]
    total = kg_ref[0].astype(F32)
    for d in range(1, N_ROW):
        total = total + kg_ref[d].astype(F32)
    frames = jnp.transpose(frame_ref[...])
    frame_ref_rows = frames
    del frame_ref_rows
    pick_q = lax.broadcasted_iota(jnp.int32, (OWN, QR + KR), 1) == (
        lax.broadcasted_iota(jnp.int32, (OWN, QR + KR), 0) + col * OWN
    )
    pick_k = lax.broadcasted_iota(jnp.int32, (OWN, QR + KR), 1) == (
        lax.broadcasted_iota(jnp.int32, (OWN, QR + KR), 0) + QR + row * OWN
    )
    pick = jnp.concatenate([pick_q, pick_k], axis=0).astype(F32).astype(BF16)
    hi, mid, lo = split3(frame_ref[...])
    own = dot(pick, hi, NT) + dot(pick, mid, NT) + dot(pick, lo, NT)
    fq = own[0:OWN]
    fk = own[OWN:]
    dgk = rotate_back(total[:, WS:F], fk, False)
    dgv = rotate_back(total[:, 512 + WS : 512 + F], fk, False)
    gk_ref[...] = jnp.concatenate([total[:, 0:WS], total[:, 512 : 512 + WS], dgk, dgv], axis=1).astype(BF16)
    msg = msg_ref[0].astype(F32)
    for d in range(1, N_COL):
        msg = msg + msg_ref[d].astype(F32)
    local = rotate_back(msg[:, WS:F], fq, True)
    head = jnp.concatenate([msg[:, 0:WS], local], axis=1).astype(BF16)
    tail = msg[:, 512:2048].astype(BF16)
    up_ref[...] = (dot(head, ow_ref[0:F]) + dot(tail, ow_ref[F:])).astype(BF16)
    dgq = rotate_back(msg[:, 2048 + WS : 2048 + F], fq, False)
    gq_ref[...] = jnp.concatenate([msg[:, 2048 : 2048 + WS], dgq], axis=1).astype(BF16)


SMEM = pl.BlockSpec(memory_space=pltpu.SMEM)
FULL = pl.BlockSpec(memory_space=pltpu.VMEM)


def params(**more):
    return pltpu.CompilerParams(vmem_limit_bytes=VMEM_LIMIT, **more)


def shape(dims, kind):
    return jax.ShapeDtypeStruct(dims, kind)


def on_device(queries, keys, frame_table, frame_index, pair_list, pair, pair_weight, point_weight, out_weight, cotangent):
    row = lax.axis_index("row")
    col = lax.axis_index("col")
    pos = jnp.stack([row, col]).astype(jnp.int32)
    codes = pair_list.reshape(CAP)
    tiles = pair.reshape(CAP, BLK, BLK, PW)
    e = jnp.asarray(head_rows(), BF16)
    gam = jnp.broadcast_to(jnp.pad(jax.nn.softplus(point_weight), (0, 4))[:, None], (16, BLK))

    key_wire = jnp.broadcast_to(keys[None], (N_ROW, OWN, 2 * F))
    key_all = lax.all_to_all(key_wire, "row", split_axis=0, concat_axis=0).reshape(KR, 2 * F)

    qf, df, dzp, frame = pl.pallas_call(
        prep_kernel,
        name="prep",
        in_specs=[SMEM] + [FULL] * 6,
        out_specs=[FULL] * 4,
        out_shape=[shape((QR, F), BF16), shape((QR, F), BF16), shape((QR, 2 * H, PW), F32), shape((16, QR + KR), F32)],
        compiler_params=params(),
        cost_estimate=pl.CostEstimate(flops=2 * QR * SW * 2016, bytes_accessed=6_000_000, transcendentals=0),
    )(pos, queries, frame_table, frame_index.reshape(1, NRES), cotangent, out_weight, pair_weight.T)

    grid = (CAP, BLK // IB)
    tile_spec = pl.BlockSpec((1, IB, BLK, PW), lambda s, i: (s, i, 0, 0))
    bz = pl.pallas_call(
        pair_in_kernel,
        name="pair_in",
        grid=grid,
        in_specs=[SMEM, tile_spec, FULL],
        out_specs=pl.BlockSpec((1, 2 * H, IB, BLK), lambda s, i: (s, 0, i, 0)),
        out_shape=shape((CAP, 2 * H, BLK, BLK), F32),
        compiler_params=params(),
        cost_estimate=pl.CostEstimate(flops=2 * CAP * BLK * BLK * PW * 32, bytes_accessed=14_000_000, transcendentals=0),
    )(codes, tiles, dzp)

    planes = (CAP, H, BLK, BLK)
    logit, da, kf, vf, stat = pl.pallas_call(
        logit_kernel,
        name="logit",
        in_specs=[SMEM] + [FULL] * 7,
        out_specs=[FULL] * 5,
        out_shape=[
            shape(planes, F32),
            shape(planes, F32),
            shape((CAP, BLK, F), BF16),
            shape((CAP, BLK, F), BF16),
            shape((32, QR), F32),
        ],
        compiler_params=params(),
    )(codes, key_all, frame, qf, df, bz, e, gam)

    stat_all = lax.all_to_all(jnp.broadcast_to(stat[None], (N_COL, 32, QR)), "col", split_axis=0, concat_axis=0)

    out = pl.pallas_call(
        out_kernel,
        name="local_out",
        grid=grid,
        in_specs=[
            SMEM,
            tile_spec,
            pl.BlockSpec((1, H, BLK, BLK), lambda s, i: (s, 0, 0, 0)),
            pl.BlockSpec((1, BLK, F), lambda s, i: (s, 0, 0)),
            FULL,
            FULL,
        ],
        out_specs=pl.BlockSpec((QR, 2048), lambda s, i: (0, 0)),
        out_shape=shape((QR, 2048), F32),
        scratch_shapes=[
            pltpu.VMEM((H, BLK, BLK), F32),
            pltpu.VMEM((H, BLK, PW), F32),
            pltpu.VMEM((BLK, HJ), BF16),
            pltpu.VMEM((HJ, F), BF16),
        ],
        compiler_params=params(),
        cost_estimate=pl.CostEstimate(flops=2 * CAP * BLK * BLK * PW * 32, bytes_accessed=14_000_000, transcendentals=0),
    )(codes, tiles, logit, vf, stat, e)

    ga, msg, kg = pl.pallas_call(
        back_kernel,
        name="back",
        in_specs=[SMEM] + [FULL] * 11,
        out_specs=[FULL] * 3,
        out_shape=[
            shape((CAP, 2 * H, BLK, BLK), F32),
            shape((QR, 2560), BF16),
            shape((KR, 1024), BF16),
        ],
        scratch_shapes=[
            pltpu.VMEM((KR, 1024), F32),
            pltpu.VMEM((BLK, HJ), BF16),
            pltpu.VMEM((HJ, BLK), BF16),
            pltpu.VMEM((HJ, BLK), BF16),
            pltpu.VMEM((HJ, F), BF16),
            pltpu.VMEM((HJ, F), BF16),
            pltpu.VMEM((HJ, F), BF16),
            pltpu.VMEM((HJ, F), BF16),
            pltpu.VMEM((QR, F), F32),
        ],
        compiler_params=params(),
    )(codes, stat_all, stat, logit, da, kf, vf, qf, df, e, gam, out)

    kg_all = lax.all_to_all(kg.reshape(N_ROW, OWN, 1024), "row", split_axis=0, concat_axis=0)
    msg_all = lax.all_to_all(msg.reshape(N_COL, OWN, 2560), "col", split_axis=0, concat_axis=0)

    grad_tiles = pl.pallas_call(
        pair_out_kernel,
        name="pair_out",
        grid=grid,
        in_specs=[SMEM, pl.BlockSpec((1, 2 * H, IB, BLK), lambda s, i: (s, 0, i, 0)), FULL],
        out_specs=tile_spec,
        out_shape=shape((CAP, BLK, BLK, PW), BF16),
        compiler_params=params(),
        cost_estimate=pl.CostEstimate(flops=2 * CAP * BLK * BLK * PW * 32, bytes_accessed=14_000_000, transcendentals=0),
    )(codes, ga, dzp)

    update, grad_queries, grad_keys = pl.pallas_call(
        final_kernel,
        name="final",
        in_specs=[SMEM] + [FULL] * 4,
        out_specs=[FULL] * 3,
        out_shape=[shape((OWN, SW), BF16), shape((OWN, F), BF16), shape((OWN, 2 * F), BF16)],
        compiler_params=params(),
    )(pos, kg_all, msg_all, frame, out_weight)
    return update, grad_queries, grad_keys, grad_tiles.reshape(pair.shape)


def solution(mesh):
    in_specs = (
        P("row", None),
        P(("col", "row"), None),
        P(),
        P(),
        P("row", "col", None),
        P("row", "col", None, None, None, None),
        P(),
        P(),
        P(),
        P("row", None),
    )
    out_specs = (
        P(("row", "col"), None),
        P(("row", "col"), None),
        P(("col", "row"), None),
        P("row", "col", None, None, None, None),
    )
    return jax.shard_map(on_device, mesh=mesh, in_specs=in_specs, out_specs=out_specs, check_vma=False)
```

```python
import functools
import math

import jax
import jax.numpy as jnp
import numpy as np
from jax import lax
from jax.experimental import pallas as pl
from jax.experimental.pallas import tpu as pltpu
from jax.sharding import PartitionSpec as P

H = 12
C = 16
PV = 8
PW = 128
BLK = 128
SW = 384
QR = 256
KR = 512
NRES = 4096
KEYB = 4
CAP = 2
F = 480
WS = 192
WP = 288
HJ = H * BLK
GJ = 6 * BLK
N_ROW = 16
N_COL = 8
OWN = 32
EMPTY = 8
NEG = -1e30
SC = 1.0 / math.sqrt(C)
WC = math.sqrt(2.0 / 72.0)
WL = math.sqrt(1.0 / 3.0)
F32 = jnp.float32
BF16 = jnp.bfloat16
MB = 1024 * 1024
G = 2
GH = 6
GF = 256
FG = G * GF
CHUNK = 32

NN = (((1,), (0,)), ((), ()))
NT = (((1,), (1,)), ((), ()))
TN = (((0,), (0,)), ((), ()))


def head_rows():
    f = np.arange(FG)
    group, at = f // GF, f % GF
    head = np.where(at < 96, at // C, ((at - 96) % 48) // PV) + GH * group
    mine = (head[None, :] == np.arange(16)[:, None]) & (at < 240)[None, :]
    scalar, point = mine & (at < 96)[None, :], mine & (at >= 96)[None, :]
    return np.concatenate([scalar, point, mine], axis=0).astype(np.float32)


def dot(a, b, dims=NN):
    return lax.dot_general(a, b, dims, preferred_element_type=F32)


def split3(x):
    hi = x.astype(BF16)
    rest = x - hi.astype(F32)
    mid = rest.astype(BF16)
    lo = (rest - mid.astype(F32)).astype(BF16)
    return hi, mid, lo


def split2(x):
    hi = x.astype(BF16)
    return hi, (x - hi.astype(F32)).astype(BF16)


def rotate(parts, frame, shift):
    out = []
    for a in range(3):
        y = sum(frame[:, 3 * a + b : 3 * a + b + 1] * parts[b] for b in range(3))
        if shift:
            y = y + frame[:, 9 + a : 10 + a]
        out.append(y)
    return out


def rotate_back(parts, frame, shift):
    if shift:
        parts = [parts[a] - frame[:, 9 + a : 10 + a] for a in range(3)]
    return [sum(frame[:, 3 * a + b : 3 * a + b + 1] * parts[a] for a in range(3)) for b in range(3)]


def components(x):
    return [x[:, 96 * b : 96 * b + 96] for b in range(3)]


def grouped(scalar, parts):
    pad = jnp.zeros((scalar.shape[0], 16), F32)
    pieces = []
    for g in range(G):
        pieces.append(scalar[:, 96 * g : 96 * g + 96])
        pieces.extend(part[:, 48 * g : 48 * g + 48] for part in parts)
        pieces.append(pad)
    return jnp.concatenate(pieces, axis=1).astype(BF16)


def ungrouped(x):
    scalar = jnp.concatenate([x[:, GF * g : GF * g + 96] for g in range(G)], axis=1)
    parts = []
    for a in range(3):
        first = 96 + 48 * a
        parts.append(jnp.concatenate([x[:, GF * g + first : GF * g + first + 48] for g in range(G)], axis=1))
    return scalar, parts


def slot_of(codes_ref, s):
    code = codes_ref[s]
    listed = code < EMPTY
    safe = jnp.where(listed, code, 0)
    return listed, safe // KEYB, safe % KEYB


def rows_of(block):
    return pl.ds(pl.multiple_of(block * BLK, BLK), BLK)


def fetch(refs, held, sems, first=0):
    copies = [pltpu.make_async_copy(ref, buf, sems.at[first + n]) for n, (ref, buf) in enumerate(zip(refs, held))]
    for copy in copies:
        copy.start()
    return copies


def look_up(table_ref, ids):
    count = ids.shape[1]
    found = jnp.zeros((48, count), F32)
    step = 512
    pad = jnp.zeros((4, step), F32)
    for first in range(0, NRES, step):
        table = jnp.concatenate([table_ref[:, first : first + step], pad], axis=0)
        table = jnp.concatenate(split3(table), axis=0)
        at = lax.broadcasted_iota(jnp.int32, (step, count), 0) + first
        found = found + dot(table, jnp.where(at == ids, 1.0, 0.0).astype(BF16))
    return found[0:16] + found[16:32] + found[32:48]


def key_kernel(keys_hbm, table_hbm, index_hbm, wire_hbm, frame_ref, held_ref, keys_ref, table_ref, index_ref, wire_ref, sems):
    copies = fetch((keys_hbm, table_hbm, index_hbm), (keys_ref, table_ref, index_ref), sems)
    for copy in copies:
        copy.wait()
    at = lax.axis_index("col") * N_ROW + lax.axis_index("row")
    window = at // 4
    ids = index_ref[:, pl.ds(pl.multiple_of(window * BLK, BLK), BLK)]
    held_ref[...] = jnp.transpose(jnp.concatenate([look_up(table_ref, ids), jnp.zeros((112, BLK), F32)], axis=0))
    frame = held_ref[pl.ds(pl.multiple_of((at % 4) * OWN, OWN), OWN), :]
    frame_ref[...] = frame
    keys = keys_ref[...].astype(F32)
    gk = rotate(components(keys[:, 2 * WS : 2 * WS + WP]), frame, True)
    gv = rotate(components(keys[:, 2 * WS + WP :]), frame, True)
    wire = jnp.concatenate([grouped(keys[:, :WS], gk), grouped(keys[:, WS : 2 * WS], gv)], axis=1)
    wire_ref[...] = wire
    copies = [pltpu.make_async_copy(wire_ref, wire_hbm.at[d], sems.at[3 + d]) for d in range(N_ROW)]
    for copy in copies:
        copy.start()
    for copy in copies:
        copy.wait()


def pair_copy(pair_ref, held, sems, k):
    rows = pl.ds(k * CHUNK, CHUNK)
    return pltpu.make_async_copy(pair_ref.at[rows], held.at[rows], sems.at[k])


CHUNKS = CAP * BLK // CHUNK


def prep_kernel(codes_ref, q_hbm, pw_hbm, gam_hbm, table_hbm, index_hbm, cot_hbm, ow_hbm, pair_ref,
                qf_hbm, df_hbm, frame_hbm, gamma_hbm, dzp_hbm, bz_hbm,
                held, sems, table_ref, index_ref, gam_ref, q_ref, cot_ref, ow_ref, pw_ref, more,
                qf_ref, df_ref, frame_ref, gamma_ref, dzp_ref, bz_ref, outs):
    loads = fetch((table_hbm, index_hbm, gam_hbm, q_hbm, cot_hbm, ow_hbm, pw_hbm),
                  (table_ref, index_ref, gam_ref, q_ref, cot_ref, ow_ref, pw_ref), more)
    for k in range(CHUNKS):
        pair_copy(pair_ref, held, sems, k).start()
    row = lax.axis_index("row")
    for copy in loads[:3]:
        copy.wait()
    frame_t = look_up(table_ref, index_ref[:, pl.ds(pl.multiple_of(row * QR, QR), QR)])
    frame = jnp.transpose(jnp.concatenate([frame_t, jnp.zeros((112, QR), F32)], axis=0))
    frame_ref[...] = frame
    raw = gam_ref[...]
    soft = jnp.maximum(raw, 0.0) + jnp.log(1.0 + jnp.exp(-jnp.abs(raw)))
    diag = lax.broadcasted_iota(jnp.int32, (16, H), 0) == lax.broadcasted_iota(jnp.int32, (16, H), 1)
    gamma_ref[...] = jnp.broadcast_to(jnp.sum(jnp.where(diag, soft, 0.0), axis=1, keepdims=True), (16, BLK))
    for copy in loads[3:]:
        copy.wait()
    q = jnp.transpose(q_ref[...].astype(F32))
    qf_ref[...] = grouped(q[:, :WS], rotate(components(q[:, WS:]), frame, True))
    cot = cot_ref[...]
    head = dot(cot, ow_ref[0:F], NT).astype(BF16).astype(F32)
    df_ref[...] = grouped(head[:, :WS], rotate(components(head[:, WS:]), frame, False))
    tail = dot(cot, ow_ref[F:], NT).astype(BF16).astype(F32)
    pwt = pw_ref[...].astype(F32)
    for h in range(H):
        dzp_ref[:, h, :] = jnp.broadcast_to(pwt[h : h + 1], (QR, PW))
        dzp_ref[:, H + h, :] = tail[:, h * PW : (h + 1) * PW]
    stores = fetch((qf_ref, df_ref, frame_ref, gamma_ref, dzp_ref), (qf_hbm, df_hbm, frame_hbm, gamma_hbm, dzp_hbm), outs, CHUNKS)

    def bz_copy(s, k):
        rows = pl.ds(k * CHUNK, CHUNK)
        return pltpu.make_async_copy(bz_ref.at[s, :, rows], bz_hbm.at[s, :, rows], outs.at[s * (BLK // CHUNK) + k])

    for s in range(CAP):
        _, qb, _ = slot_of(codes_ref, s)

        def some(k, carry, s=s, qb=qb):
            @pl.when(k % (CHUNK // 16) == 0)
            def _():
                rows = pl.ds(pl.multiple_of(s * BLK + k * 16, 16), CHUNK)
                pltpu.make_async_copy(pair_ref.at[rows], held.at[rows], sems.at[s * (BLK // CHUNK) + k // (CHUNK // 16)]).wait()

            first = k * 16
            for i in range(0, 16, 2):
                lhs = dzp_ref[pl.ds(qb * BLK + first + i, 2)].reshape(4 * H, PW).astype(BF16)
                z = held[pl.ds(s * BLK + first + i, 2)].reshape(2 * BLK, PW)
                found = dot(lhs, z, NT)
                bz_ref[s, :, first + i, :] = found[0 : 2 * H, 0:BLK]
                bz_ref[s, :, first + i + 1, :] = found[2 * H :, BLK:]

            @pl.when(k % (CHUNK // 16) == CHUNK // 16 - 1)
            def _():
                bz_copy(s, k // (CHUNK // 16)).start()

            return carry

        lax.fori_loop(0, BLK // 16, some, 0)
    for copy in stores:
        copy.wait()
    for s in range(CAP):
        for k in range(BLK // CHUNK):
            bz_copy(s, k).wait()


def logit_kernel(codes_ref, keys_hbm, qf_hbm, df_hbm, e_hbm, gam_hbm, bz_hbm, mine_hbm, logit_hbm, da_hbm, stat_hbm,
                 keys_ref, qf_ref, df_ref, e_ref, gam_ref, mine_ref, bz_ref, logit_ref, da_ref, ins, outs):
    places = [slot_of(codes_ref, s) for s in range(CAP)]
    small = fetch((e_hbm, gam_hbm), (e_ref, gam_ref), ins)
    loads = []
    for s, (_, qb, kb) in enumerate(places):
        loads.append(fetch(
            (keys_hbm.at[rows_of(kb)], qf_hbm.at[rows_of(qb)], df_hbm.at[rows_of(qb)], bz_hbm.at[s]),
            (keys_ref.at[s], qf_ref.at[s], df_ref.at[s], bz_ref.at[s]), ins, 2 + 4 * s,
        ))
    stores = []
    for copy in small:
        copy.wait()
    e = e_ref[...]
    lane = lax.broadcasted_iota(jnp.int32, (BLK, BLK), 1)
    stats = []
    for s in range(CAP):
        listed, qb, kb = places[s]
        for copy in loads[s][:3]:
            copy.wait()
        kf = keys_ref[s, :, 0:FG]
        vf = keys_ref[s, :, FG:]
        qf = qf_ref[s]
        df = df_ref[s]
        qhi, qlo = split2(jnp.square(qf.astype(F32)))
        khi, klo = split2(jnp.square(kf.astype(F32)))
        ep = e[16:32]
        qn = dot(qhi, ep, NT) + dot(qlo, ep, NT)
        kn = dot(ep, khi, NT) + dot(ep, klo, NT)
        held = jnp.zeros((BLK, BLK), F32)
        loads[s][3].wait()
        for h in range(0, H, 2):
            at = slice(h // GH * GF, h // GH * GF + GF)
            kg = kf[:, at]
            vg = vf[:, at]
            qg = qf[:, at]
            das = dot(df[:, at], jnp.concatenate([vg * e[32 + h : 33 + h, at], vg * e[33 + h : 34 + h, at]], axis=0), NT)
            for n in range(2):
                u = h + n
                both = dot(qg, jnp.concatenate([kg * e[u : u + 1, at], kg * e[16 + u : 17 + u, at]], axis=0), NT)
                dist = qn[:, u : u + 1] + kn[u : u + 1, :] - 2.0 * both[:, BLK:]
                logit = (WL * SC) * both[:, :BLK] + WL * bz_ref[s, u] - (0.5 * WL * WC) * gam_ref[u : u + 1] * dist
                da = bz_ref[s, H + u] + das[:, n * BLK : (n + 1) * BLK]
                logit_ref[s, u] = logit
                da_ref[s, u] = da
                top = jnp.max(logit, axis=1, keepdims=True)
                p = jnp.exp(logit - top)
                total = jnp.sum(p, axis=1, keepdims=True)
                mean = jnp.sum(p * da, axis=1, keepdims=True) / total
                held = jnp.where(lane == u, top + jnp.log(total), held)
                held = jnp.where(lane == 16 + u, mean, held)
            if h % 4 == 2:
                some = pl.ds(h - 2, 4)
                for n, (ref, hbm) in enumerate(((logit_ref, logit_hbm), (da_ref, da_hbm))):
                    at = (2 * s + n) * (H // 4) + h // 4
                    stores.append(pltpu.make_async_copy(ref.at[s, some], hbm.at[s, some], outs.at[at]))
                    stores[-1].start()
        stats.append((listed, qb, jnp.transpose(held)))
    for b in range(2):
        lse = []
        for listed, qb, held in stats:
            lse.append(jnp.where(jnp.logical_and(listed, qb == b), held[0:16], NEG))
        top = jnp.maximum(lse[0], lse[1])
        w0 = jnp.exp(lse[0] - top)
        w1 = jnp.exp(lse[1] - top)
        total = w0 + w1
        merged = jnp.concatenate(
            [top + jnp.log(total), (w0 * stats[0][2][16:32] + w1 * stats[1][2][16:32]) / total], axis=0
        )
        mine_ref[:, b * BLK : (b + 1) * BLK] = merged
    stores.extend(fetch([mine_ref] * (N_COL + 1), [mine_hbm] + [stat_hbm.at[d] for d in range(N_COL)], ins))
    for copy in stores:
        copy.wait()


def out_kernel(codes_ref, pair_ref, logit_hbm, keys_hbm, stat_hbm, e_hbm, o_hbm, held, p_ref, nz_ref, cat_ref, bd_ref, sems,
               logit_ref, keys_ref, stat_ref, e_ref, o_ref, ins):
    places = [slot_of(codes_ref, s) for s in range(CAP)]
    loads = fetch((stat_hbm, e_hbm), (stat_ref, e_ref), ins)
    for s, (_, _, kb) in enumerate(places):
        loads.extend(fetch((logit_hbm.at[s], keys_hbm.at[rows_of(kb), pl.ds(FG, FG)]), (logit_ref.at[s], keys_ref.at[s]), ins, 2 + 2 * s))
    for k in range(CHUNKS):
        pair_copy(pair_ref, held, sems, k).start()
    loads[0].wait()
    loads[1].wait()
    o_ref[...] = jnp.zeros_like(o_ref)
    for s in range(CAP):
        listed, qb, kb = places[s]
        lse = jnp.transpose(jnp.concatenate([stat_ref[:, rows_of(qb)], jnp.zeros((96, BLK), F32)], axis=0))
        lse = jnp.where(listed, lse, -NEG)
        loads[2 + 2 * s].wait()
        loads[3 + 2 * s].wait()
        vf = keys_ref[s]
        for h in range(H):
            at = slice(h // GH * GF, h // GH * GF + GF)
            p = jnp.exp(logit_ref[s, h] - lse[:, h : h + 1])
            p_ref[h] = p
            cat_ref[:, h * BLK : (h + 1) * BLK] = p.astype(BF16)
            bd_ref[h * BLK : (h + 1) * BLK, :] = vf[:, at] * e_ref[32 + h : 33 + h, at]
        for g in range(G):
            at = slice(g * GJ, (g + 1) * GJ)
            o_ref[rows_of(qb), g * GF : (g + 1) * GF] += dot(cat_ref[:, at], bd_ref[at, :])

        def some(k, carry, s=s):
            @pl.when(k % (CHUNK // 16) == 0)
            def _():
                rows = pl.ds(pl.multiple_of(s * BLK + k * 16, 16), CHUNK)
                pltpu.make_async_copy(pair_ref.at[rows], held.at[rows], sems.at[s * (BLK // CHUNK) + k // (CHUNK // 16)]).wait()

            first = k * 16
            zero = jnp.zeros((H, BLK), F32)
            for i in range(0, 16, 2):
                w = jnp.concatenate(
                    [
                        jnp.concatenate([p_ref[:, first + i, :], zero], axis=1),
                        jnp.concatenate([zero, p_ref[:, first + i + 1, :]], axis=1),
                    ],
                    axis=0,
                ).astype(BF16)
                found = dot(w, held[pl.ds(s * BLK + first + i, 2)].reshape(2 * BLK, PW))
                nz_ref[:, first + i, :] = found[0:H]
                nz_ref[:, first + i + 1, :] = found[H:]
            return carry

        lax.fori_loop(0, BLK // 16, some, 0)
        for h in range(H):
            o_ref[rows_of(qb), FG + h * PW : FG + (h + 1) * PW] += nz_ref[h]
    (copy,) = fetch((o_ref,), (o_hbm,), ins)
    copy.wait()


def back_kernel(codes_ref, stat_hbm, stats_hbm, keys_hbm, qf_hbm, df_hbm, e_hbm, gam_hbm, logit_hbm, da_hbm, o_hbm,
                whole_hbm, keep_hbm, kg_hbm, send_hbm,
                mine_ref, all_ref, keys_ref, qf_ref, df_ref, e_ref, gam_ref, logit_ref, da_ref, o_ref, ins,
                whole_ref, keep_ref, kg_ref, send_ref, sems, kg_acc, gcat, gstk, astk, kbd, qbd, dbd, ebd, dq_acc, msg):
    places = [slot_of(codes_ref, s) for s in range(CAP)]
    small = fetch((stat_hbm, stats_hbm, e_hbm, gam_hbm), (mine_ref, all_ref, e_ref, gam_ref), ins)
    loads = []
    for s, (_, qb, kb) in enumerate(places):
        loads.append(fetch(
            (logit_hbm.at[s], da_hbm.at[s], keys_hbm.at[rows_of(kb), pl.ds(0, FG)], qf_hbm.at[rows_of(qb)], df_hbm.at[rows_of(qb)]),
            (logit_ref.at[s], da_ref.at[s], keys_ref.at[s], qf_ref.at[s], df_ref.at[s]), ins, 10 + 5 * s,
        ))
    (o_copy,) = fetch((o_hbm,), (o_ref,), ins, 20)
    for copy in small:
        copy.wait()
    held = [all_ref[d] for d in range(N_COL)]
    top = held[0][0:16]
    for d in range(1, N_COL):
        top = jnp.maximum(top, held[d][0:16])
    total = jnp.zeros((16, QR), F32)
    mean = jnp.zeros((16, QR), F32)
    for d in range(N_COL):
        w = jnp.exp(held[d][0:16] - top)
        total = total + w
        mean = mean + w * held[d][16:32]
    lse = top + jnp.log(total)
    delta = mean / total
    alpha = jnp.exp(mine_ref[0:16] - lse)
    whole_t = jnp.concatenate([lse, delta, alpha, jnp.zeros((80, QR), F32)], axis=0)
    whole = jnp.transpose(whole_t)
    whole_ref[...] = whole
    e = e_ref[32:48]
    gam_f = jnp.sum(e.astype(F32) * gam_ref[:, 0:1], axis=0, keepdims=True)
    point = jnp.sum(e_ref[16:32].astype(F32), axis=0, keepdims=True)
    scalar = jnp.sum(e_ref[0:16].astype(F32), axis=0, keepdims=True)
    fa = WC * gam_f * point + SC * scalar
    fb = -WC * gam_f * point
    kg_acc[...] = jnp.zeros_like(kg_acc)
    dq_acc[...] = jnp.zeros_like(dq_acc)
    for h in range(H):
        at = slice(h // GH * GF, h // GH * GF + GF)
        ebd[h * BLK : (h + 1) * BLK, :] = jnp.broadcast_to(e[h : h + 1, at], (BLK, GF))
    for s in range(CAP):
        listed, qb, kb = places[s]
        for copy in loads[s]:
            copy.wait()
        stat = jnp.where(qb == 0, whole[0:BLK], whole[BLK:])
        lse_s = jnp.where(listed, stat, -NEG)
        kf = keys_ref[s]
        qf = qf_ref[s]
        df = df_ref[s]
        for h in range(H):
            at = slice(h // GH * GF, h // GH * GF + GF)
            block = slice(h * BLK, (h + 1) * BLK)
            a = jnp.exp(logit_ref[s, h] - lse_s[:, h : h + 1])
            g = WL * a * (da_ref[s, h] - stat[:, 16 + h : 17 + h])
            gr = g.astype(BF16)
            gcat[:, block] = gr
            gstk[block, :] = gr
            astk[block, :] = a.astype(BF16)
            eh = e[h : h + 1, at]
            kbd[block, :] = kf[:, at] * eh
            qbd[block, :] = qf[:, at] * eh
            dbd[block, :] = df[:, at] * eh
        for g in range(G):
            at = slice(g * GF, (g + 1) * GF)
            block = slice(g * GJ, (g + 1) * GJ)
            dq_raw = dot(gcat[:, block], kbd[block, :])
            row_sum = dot(gcat[:, block], ebd[block, :])
            dq_acc[rows_of(qb), at] += fa[:, at] * dq_raw + fb[:, at] * row_sum * qf[:, at].astype(F32)
            dk_raw = dot(gstk[block, :], qbd[block, :], TN)
            col_sum = dot(gstk[block, :], ebd[block, :], TN)
            kg_acc[rows_of(kb), at] += fa[:, at] * dk_raw + fb[:, at] * col_sum * kf[:, at].astype(F32)
            kg_acc[rows_of(kb), FG + g * GF : FG + (g + 1) * GF] += dot(astk[block, :], dbd[block, :], TN)
    kg_ref[...] = kg_acc[...].astype(BF16)
    kg_copy = pltpu.make_async_copy(kg_ref, kg_hbm, sems.at[0])
    kg_copy.start()
    o_copy.wait()
    ahi, alo = split2(whole[:, 32:48])
    msg[:, 0:FG] = (o_ref[:, 0:FG] * (dot(ahi, e) + dot(alo, e))).astype(BF16)
    for h in range(H):
        at = slice(FG + h * PW, FG + (h + 1) * PW)
        msg[:, at] = (o_ref[:, at] * whole[:, 32 + h : 33 + h]).astype(BF16)
    msg[:, 2048:] = dq_acc[...].astype(BF16)
    core = lax.axis_index("col") % 2
    for x in range(4):
        keep_ref[x] = msg[pl.ds(pl.multiple_of((2 * x + core) * OWN, OWN), OWN), :]
        send_ref[x] = msg[pl.ds(pl.multiple_of((2 * x + 1 - core) * OWN, OWN), OWN), :]
    copies = fetch((send_ref, keep_ref, whole_ref), (send_hbm, keep_hbm, whole_hbm), sems, 1)
    for copy in [kg_copy] + copies:
        copy.wait()


def fold_kernel(keep_ref, got_ref, own_ref, one_ref, two_ref, three_ref):
    x = lax.axis_index("col") // 2
    for k, ref in enumerate((own_ref, one_ref, two_ref, three_ref)):
        at = (x + k) % 4
        ref[...] = (keep_ref[at].astype(F32) + got_ref[at].astype(F32)).astype(BF16)


def pair_out_kernel(codes_ref, whole_hbm, logit_hbm, da_hbm, dzp_hbm, out_ref, held, ga, sems, logit_ref, da_ref, dzp_ref, whole_ref, ins):
    (whole_copy,) = fetch((whole_hbm,), (whole_ref,), ins, 2 * CAP + 1)
    loads = []
    for s in range(CAP):
        loads.append(pltpu.make_async_copy(logit_hbm.at[s], logit_ref.at[s], ins.at[2 * s]))
        loads.append(pltpu.make_async_copy(da_hbm.at[s], da_ref.at[s], ins.at[2 * s + 1]))
    loads.insert(2, pltpu.make_async_copy(dzp_hbm, dzp_ref, ins.at[2 * CAP]))
    for copy in loads:
        copy.start()
    whole_copy.wait()
    for s in range(CAP):
        listed, qb, _ = slot_of(codes_ref, s)
        stat = whole_ref[rows_of(qb), :]
        lse_s = jnp.where(listed, stat, -NEG)
        for copy in loads[0:2] if s == 0 else loads[3:5]:
            copy.wait()
        for h in range(H):
            a = jnp.exp(logit_ref[s, h] - lse_s[:, h : h + 1])
            ga[h] = WL * a * (da_ref[s, h] - stat[:, 16 + h : 17 + h])
            ga[H + h] = a
        if s == 0:
            loads[2].wait()

        def some(k, carry, s=s, qb=qb):
            first = k * 16
            zero = jnp.zeros((2 * H, PW), BF16)
            for i in range(0, 16, 2):
                lhs = jnp.concatenate([ga[:, first + i, :], ga[:, first + i + 1, :]], axis=0).astype(BF16)
                one = dzp_ref[qb * BLK + first + i].astype(BF16)
                two = dzp_ref[qb * BLK + first + i + 1].astype(BF16)
                rhs = jnp.concatenate(
                    [jnp.concatenate([one, zero], axis=1), jnp.concatenate([zero, two], axis=1)], axis=0
                )
                found = dot(lhs, rhs, TN).astype(BF16)
                held[s * BLK + first + i] = found[:, :PW]
                held[s * BLK + first + i + 1] = found[:, PW:]

            @pl.when(k % (CHUNK // 16) == CHUNK // 16 - 1)
            def _():
                rows = pl.ds(pl.multiple_of(s * BLK + k * 16 + 16 - CHUNK, 16), CHUNK)
                pltpu.make_async_copy(held.at[rows], out_ref.at[rows], sems.at[s * (BLK // CHUNK) + k // (CHUNK // 16)]).start()

            return carry

        lax.fori_loop(0, BLK // 16, some, 0)
    for k in range(CHUNKS):
        pair_copy(held, out_ref, sems, k).wait()


def final_kernel(kg_ref, own_ref, one_ref, two_ref, three_ref, frame_q_ref, frame_k_ref, ow_hbm, up_ref, gq_ref, gk_ref, ow_ref, sems):
    (ow_copy,) = fetch((ow_hbm,), (ow_ref,), sems)
    total = kg_ref[0].astype(F32)
    for d in range(1, N_ROW):
        total = total + kg_ref[d].astype(F32)
    fk = frame_k_ref[...]
    fq = frame_q_ref[pl.ds(pl.multiple_of(lax.axis_index("col") * OWN, OWN), OWN), :]
    dk, dgk = ungrouped(total[:, :FG])
    dv, dgv = ungrouped(total[:, FG:])
    gk_ref[...] = jnp.concatenate(
        [dk, dv] + rotate_back(dgk, fk, False) + rotate_back(dgv, fk, False), axis=1
    ).astype(BF16)
    msg = (own_ref[...].astype(F32) + one_ref[...].astype(F32)) + (two_ref[...].astype(F32) + three_ref[...].astype(F32))
    scalar, parts = ungrouped(msg[:, :FG])
    head = jnp.concatenate([scalar] + rotate_back(parts, fq, True), axis=1).astype(BF16)
    tail = msg[:, FG:2048].astype(BF16)
    ow_copy.wait()
    up_ref[...] = (dot(head, ow_ref[0:F]) + dot(tail, ow_ref[F:])).astype(BF16)
    dq, dgq = ungrouped(msg[:, 2048:])
    gq_ref[...] = jnp.concatenate([dq] + rotate_back(dgq, fq, False), axis=1).astype(BF16)


SMEM = pl.BlockSpec(memory_space=pltpu.SMEM)
FULL = pl.BlockSpec(memory_space=pltpu.VMEM)
HBM = pl.BlockSpec(memory_space=pltpu.HBM)
DMA = pltpu.SemaphoreType.DMA


def call(kernel, name, ins, outs, scratch, mb, flops=0, nbytes=0):
    return pl.pallas_call(
        kernel,
        name=name,
        in_specs=ins,
        out_specs=[spec for _, spec in outs],
        out_shape=[shape for shape, _ in outs],
        scratch_shapes=scratch,
        compiler_params=pltpu.CompilerParams(vmem_limit_bytes=56 * MB if mb > 12 else mb * MB),
        cost_estimate=pl.CostEstimate(flops=flops, bytes_accessed=nbytes, transcendentals=0),
    )


def near(dims, kind):
    return jax.ShapeDtypeStruct(dims, kind), FULL


def far(dims, kind):
    return jax.ShapeDtypeStruct(dims, kind), HBM


def free(dims, kind):
    return jax.ShapeDtypeStruct(dims, kind), FULL


def on_device(queries, keys, frame_table, frame_index, pair_list, pair, pair_weight, point_weight, out_weight, cotangent):
    codes = pair_list.reshape(CAP)
    tiles = pair.reshape(CAP * BLK, BLK, PW)
    e = jnp.asarray(head_rows(), BF16)
    index = frame_index.reshape(1, NRES)
    sems = DMA((CHUNKS,))
    held = pltpu.VMEM((CAP * BLK, BLK, PW), BF16)
    table = pltpu.VMEM((12, NRES), F32)
    where = pltpu.VMEM((1, NRES), jnp.int32)
    planes = (CAP, H, BLK, BLK)

    key_wire, frame_k = call(
        key_kernel, "keys", [HBM] * 3, [far((N_ROW, OWN, 2 * FG), BF16), near((OWN, BLK), F32)],
        [pltpu.VMEM((BLK, BLK), F32), pltpu.VMEM((OWN, 2 * F), BF16), table, where, pltpu.VMEM((OWN, 2 * FG), BF16),
         DMA((3 + N_ROW,))], 56,
    )(keys, frame_table, index)
    key_all = lax.all_to_all(key_wire, "row", split_axis=0, concat_axis=0).reshape(KR, 2 * FG)

    half = pltpu.VMEM((CAP, BLK, FG), BF16)
    marks = pltpu.VMEM((48, FG), BF16)
    gammas = pltpu.VMEM((16, BLK), F32)
    rows = pltpu.VMEM((QR, FG), BF16)
    plane_buf = pltpu.VMEM(planes, F32)
    dzp_buf = pltpu.VMEM((QR, 2 * H, PW), F32)
    bz_buf = pltpu.VMEM((CAP, 2 * H, BLK, BLK), F32)
    qf, df, frame_q, gam, dzp, bz = call(
        prep_kernel, "prep", [SMEM] + [HBM] * 8,
        [far((QR, FG), BF16), far((QR, FG), BF16), far((QR, BLK), F32), far((16, BLK), F32),
         far((QR, 2 * H, PW), F32), far((CAP, 2 * H, BLK, BLK), F32)],
        [held, sems, table, where, pltpu.VMEM((1, H), F32), pltpu.VMEM((F, QR), BF16), pltpu.VMEM((QR, SW), BF16),
         pltpu.VMEM((2016, SW), BF16), pltpu.VMEM((H, PW), BF16), DMA((7,)),
         rows, rows, pltpu.VMEM((QR, BLK), F32), gammas, dzp_buf, bz_buf, DMA((CHUNKS + 5,))],
        56, flops=3_000_000_000, nbytes=30_000_000,
    )(codes, queries.T, pair_weight.T, point_weight.reshape(1, H), frame_table, index, cotangent, out_weight, tiles)

    mine, logit, da, stat = call(
        logit_kernel, "logit", [SMEM] + [HBM] * 6, [far((32, QR), F32), far(planes, F32), far(planes, F32), far((N_COL, 32, QR), F32)],
        [pltpu.VMEM((CAP, BLK, 2 * FG), BF16), half, half, marks, gammas, pltpu.VMEM((32, QR), F32), bz_buf, plane_buf,
         plane_buf, DMA((10,)), DMA((H,))], 56,
    )(codes, key_all, qf, df, e, gam, bz)

    stat_all = lax.all_to_all(stat, "col", split_axis=0, concat_axis=0)

    (out,) = call(
        out_kernel, "local_out", [SMEM] + [HBM] * 5, [far((QR, 2048), F32)],
        [held, pltpu.VMEM((H, BLK, BLK), F32), pltpu.VMEM((H, BLK, PW), F32), pltpu.VMEM((BLK, HJ), BF16),
         pltpu.VMEM((HJ, GF), BF16), sems, plane_buf, half, pltpu.VMEM((32, QR), F32), marks,
         pltpu.VMEM((QR, 2048), F32), DMA((6,))], 56, flops=2_000_000_000, nbytes=20_000_000,
    )(codes, tiles, logit, key_all, mine, e)

    whole, keep, kg, send = call(
        back_kernel, "back", [SMEM] + [HBM] * 10,
        [far((QR, BLK), F32), far((4, OWN, 2560), BF16), far((KR, 2 * FG), BF16), far((4, OWN, 2560), BF16)],
        [pltpu.VMEM((32, QR), F32), pltpu.VMEM((N_COL, 32, QR), F32), half, half, half, marks, gammas, plane_buf, plane_buf,
         pltpu.VMEM((QR, 2048), F32), DMA((21,)),
         pltpu.VMEM((QR, BLK), F32), pltpu.VMEM((4, OWN, 2560), BF16), pltpu.VMEM((KR, 2 * FG), BF16),
         pltpu.VMEM((4, OWN, 2560), BF16), DMA((4,)),
         pltpu.VMEM((KR, 2 * FG), F32), pltpu.VMEM((BLK, HJ), BF16), pltpu.VMEM((HJ, BLK), BF16),
         pltpu.VMEM((HJ, BLK), BF16), pltpu.VMEM((HJ, GF), BF16), pltpu.VMEM((HJ, GF), BF16),
         pltpu.VMEM((HJ, GF), BF16), pltpu.VMEM((HJ, GF), BF16), pltpu.VMEM((QR, FG), F32),
         pltpu.VMEM((QR, 2560), BF16)], 56,
    )(codes, mine, stat_all, key_all, qf, df, e, gam, logit, da, out)

    kg_all = lax.all_to_all(kg.reshape(N_ROW, OWN, 2 * FG), "row", split_axis=0, concat_axis=0)
    got = lax.ppermute(send, "col", [(d, d ^ 1) for d in range(N_COL)])
    own, *away = call(
        fold_kernel, "fold", [FULL] * 2, [near((OWN, 2560), BF16)] + [free((OWN, 2560), BF16)] * 3, [], 4
    )(keep, got)
    came = [
        lax.ppermute(part, "col", [(d, (d + 2 * k) % N_COL) for d in range(N_COL)])
        for k, part in enumerate(away, 1)
    ]

    (grad_tiles,) = call(
        pair_out_kernel, "pair_out", [SMEM] + [HBM] * 4, [far((CAP * BLK, BLK, PW), BF16)],
        [held, pltpu.VMEM((2 * H, BLK, BLK), F32), sems, plane_buf, plane_buf, dzp_buf,
         pltpu.VMEM((QR, BLK), F32), DMA((2 * CAP + 2,))], 56, flops=4_000_000_000, nbytes=30_000_000,
    )(codes, whole, logit, da, dzp)

    update, grad_queries, grad_keys = call(
        final_kernel, "final", [FULL] * 7 + [HBM],
        [free((OWN, SW), BF16), free((OWN, F), BF16), free((OWN, 2 * F), BF16)],
        [pltpu.VMEM((2016, SW), BF16), DMA((1,))], 12,
    )(kg_all, own, *came, frame_q, frame_k, out_weight)
    return update, grad_queries, grad_keys, grad_tiles.reshape(pair.shape)


def solution(mesh):
    in_specs = (
        P("row", None),
        P(("col", "row"), None),
        P(),
        P(),
        P("row", "col", None),
        P("row", "col", None, None, None, None),
        P(),
        P(),
        P(),
        P("row", None),
    )
    out_specs = (
        P(("row", "col"), None),
        P(("row", "col"), None),
        P(("col", "row"), None),
        P("row", "col", None, None, None, None),
    )
    return jax.shard_map(on_device, mesh=mesh, in_specs=in_specs, out_specs=out_specs, check_vma=False)
```

```python
import functools
import math

import jax
import jax.numpy as jnp
import numpy as np
from jax import lax
from jax.experimental import pallas as pl
from jax.experimental.pallas import tpu as pltpu
from jax.sharding import PartitionSpec as P

H = 12
C = 16
PV = 8
PW = 128
BLK = 128
SW = 384
QR = 256
KR = 512
NRES = 4096
KEYB = 4
CAP = 2
F = 480
WS = 192
WP = 288
HJ = H * BLK
GJ = 6 * BLK
N_ROW = 16
N_COL = 8
OWN = 32
EMPTY = 8
NEG = -1e30
SC = 1.0 / math.sqrt(C)
WC = math.sqrt(2.0 / 72.0)
WL = math.sqrt(1.0 / 3.0)
F32 = jnp.float32
BF16 = jnp.bfloat16
MB = 1024 * 1024
G = 2
GH = 6
GF = 256
FG = G * GF
CHUNK = 32
STEP = 64

NN = (((1,), (0,)), ((), ()))
NT = (((1,), (1,)), ((), ()))
TN = (((0,), (0,)), ((), ()))


def head_rows():
    f = np.arange(FG)
    group, at = f // GF, f % GF
    head = np.where(at < 96, at // C, ((at - 96) % 48) // PV) + GH * group
    mine = (head[None, :] == np.arange(16)[:, None]) & (at < 240)[None, :]
    scalar, point = mine & (at < 96)[None, :], mine & (at >= 96)[None, :]
    return np.concatenate([scalar, point, mine], axis=0).astype(np.float32)


def dot(a, b, dims=NN):
    return lax.dot_general(a, b, dims, preferred_element_type=F32)


def split3(x):
    hi = x.astype(BF16)
    rest = x - hi.astype(F32)
    mid = rest.astype(BF16)
    lo = (rest - mid.astype(F32)).astype(BF16)
    return hi, mid, lo


def split2(x):
    hi = x.astype(BF16)
    return hi, (x - hi.astype(F32)).astype(BF16)


def rotate(parts, frame, shift):
    out = []
    for a in range(3):
        y = sum(frame[:, 3 * a + b : 3 * a + b + 1] * parts[b] for b in range(3))
        if shift:
            y = y + frame[:, 9 + a : 10 + a]
        out.append(y)
    return out


def rotate_back(parts, frame, shift):
    if shift:
        parts = [parts[a] - frame[:, 9 + a : 10 + a] for a in range(3)]
    return [sum(frame[:, 3 * a + b : 3 * a + b + 1] * parts[a] for a in range(3)) for b in range(3)]


def components(x):
    return [x[:, 96 * b : 96 * b + 96] for b in range(3)]


def grouped(scalar, parts):
    pad = jnp.zeros((scalar.shape[0], 16), F32)
    pieces = []
    for g in range(G):
        pieces.append(scalar[:, 96 * g : 96 * g + 96])
        pieces.extend(part[:, 48 * g : 48 * g + 48] for part in parts)
        pieces.append(pad)
    return jnp.concatenate(pieces, axis=1).astype(BF16)


def ungrouped(x):
    scalar = jnp.concatenate([x[:, GF * g : GF * g + 96] for g in range(G)], axis=1)
    parts = []
    for a in range(3):
        first = 96 + 48 * a
        parts.append(jnp.concatenate([x[:, GF * g + first : GF * g + first + 48] for g in range(G)], axis=1))
    return scalar, parts


def slot_of(codes_ref, s):
    code = codes_ref[s]
    listed = code < EMPTY
    safe = jnp.where(listed, code, 0)
    return listed, safe // KEYB, safe % KEYB


def rows_of(block):
    return pl.ds(pl.multiple_of(block * BLK, BLK), BLK)


def fetch(refs, held, sems, first=0):
    copies = [pltpu.make_async_copy(ref, buf, sems.at[first + n]) for n, (ref, buf) in enumerate(zip(refs, held))]
    for copy in copies:
        copy.start()
    return copies


def look_up(table_ref, ids):
    count = ids.shape[1]
    found = jnp.zeros((48, count), F32)
    step = 512
    pad = jnp.zeros((4, step), F32)
    for first in range(0, NRES, step):
        table = jnp.concatenate([table_ref[:, first : first + step], pad], axis=0)
        table = jnp.concatenate(split3(table), axis=0)
        at = lax.broadcasted_iota(jnp.int32, (step, count), 0) + first
        found = found + dot(table, jnp.where(at == ids, 1.0, 0.0).astype(BF16))
    return found[0:16] + found[16:32] + found[32:48]


def key_kernel(keys_hbm, table_hbm, index_hbm, wire_hbm, frame_ref, held_ref, keys_ref, table_ref, index_ref, wire_ref, sems):
    copies = fetch((keys_hbm, table_hbm, index_hbm), (keys_ref, table_ref, index_ref), sems)
    for copy in copies:
        copy.wait()
    at = lax.axis_index("col") * N_ROW + lax.axis_index("row")
    window = at // 4
    ids = index_ref[:, pl.ds(pl.multiple_of(window * BLK, BLK), BLK)]
    held_ref[...] = jnp.transpose(jnp.concatenate([look_up(table_ref, ids), jnp.zeros((112, BLK), F32)], axis=0))
    frame = held_ref[pl.ds(pl.multiple_of((at % 4) * OWN, OWN), OWN), :]
    frame_ref[...] = frame
    keys = keys_ref[...].astype(F32)
    gk = rotate(components(keys[:, 2 * WS : 2 * WS + WP]), frame, True)
    gv = rotate(components(keys[:, 2 * WS + WP :]), frame, True)
    wire = jnp.concatenate([grouped(keys[:, :WS], gk), grouped(keys[:, WS : 2 * WS], gv)], axis=1)
    wire_ref[...] = wire
    copies = [pltpu.make_async_copy(wire_ref, wire_hbm.at[d], sems.at[3 + d]) for d in range(N_ROW)]
    for copy in copies:
        copy.start()
    for copy in copies:
        copy.wait()


def pair_copy(pair_ref, held, sems, k):
    rows = pl.ds(k * CHUNK, CHUNK)
    return pltpu.make_async_copy(pair_ref.at[rows], held.at[rows], sems.at[k])


CHUNKS = CAP * BLK // CHUNK


def prep_kernel(codes_ref, q_hbm, pw_hbm, gam_hbm, table_hbm, index_hbm, cot_hbm, ow_hbm, pair_ref,
                qf_hbm, df_hbm, frame_hbm, gamma_hbm, dzp_hbm, bz_hbm,
                held, sems, table_ref, index_ref, gam_ref, q_ref, cot_ref, ow_ref, pw_ref, more,
                qf_ref, df_ref, frame_ref, gamma_ref, dzp_ref, bz_ref, outs):
    loads = fetch((table_hbm, index_hbm, gam_hbm, q_hbm, cot_hbm, ow_hbm, pw_hbm),
                  (table_ref, index_ref, gam_ref, q_ref, cot_ref, ow_ref, pw_ref), more)
    for k in range(CHUNKS):
        pair_copy(pair_ref, held, sems, k).start()
    row = lax.axis_index("row")
    for copy in loads[:3]:
        copy.wait()
    frame_t = look_up(table_ref, index_ref[:, pl.ds(pl.multiple_of(row * QR, QR), QR)])
    frame = jnp.transpose(jnp.concatenate([frame_t, jnp.zeros((112, QR), F32)], axis=0))
    frame_ref[...] = frame
    raw = gam_ref[...]
    soft = jnp.maximum(raw, 0.0) + jnp.log(1.0 + jnp.exp(-jnp.abs(raw)))
    diag = lax.broadcasted_iota(jnp.int32, (16, H), 0) == lax.broadcasted_iota(jnp.int32, (16, H), 1)
    gamma_ref[...] = jnp.broadcast_to(jnp.sum(jnp.where(diag, soft, 0.0), axis=1, keepdims=True), (16, BLK))
    for copy in loads[3:]:
        copy.wait()
    q = jnp.transpose(q_ref[...].astype(F32))
    qf_ref[...] = grouped(q[:, :WS], rotate(components(q[:, WS:]), frame, True))
    cot = cot_ref[...]
    head = dot(cot, ow_ref[0:F], NT).astype(BF16).astype(F32)
    df_ref[...] = grouped(head[:, :WS], rotate(components(head[:, WS:]), frame, False))
    tail = dot(cot, ow_ref[F:], NT).astype(BF16).astype(F32)
    pwt = pw_ref[...].astype(F32)
    for h in range(H):
        dzp_ref[:, h, :] = jnp.broadcast_to(pwt[h : h + 1], (QR, PW))
        dzp_ref[:, H + h, :] = tail[:, h * PW : (h + 1) * PW]
    stores = fetch((qf_ref, df_ref, frame_ref, gamma_ref, dzp_ref), (qf_hbm, df_hbm, frame_hbm, gamma_hbm, dzp_hbm), outs, CHUNKS)

    def bz_copy(s, k):
        rows = pl.ds(k * CHUNK, CHUNK)
        return pltpu.make_async_copy(bz_ref.at[s, :, rows], bz_hbm.at[s, :, rows], outs.at[s * (BLK // CHUNK) + k])

    for s in range(CAP):
        _, qb, _ = slot_of(codes_ref, s)

        def some(k, carry, s=s, qb=qb):
            for c in range(STEP // CHUNK):
                rows = pl.ds(pl.multiple_of(s * BLK + k * STEP + c * CHUNK, CHUNK), CHUNK)
                at = s * (BLK // CHUNK) + k * (STEP // CHUNK) + c
                pltpu.make_async_copy(pair_ref.at[rows], held.at[rows], sems.at[at]).wait()
            first = k * STEP
            for i in range(0, STEP, 2):
                lhs = dzp_ref[pl.ds(qb * BLK + first + i, 2)].reshape(4 * H, PW).astype(BF16)
                z = held[pl.ds(s * BLK + first + i, 2)].reshape(2 * BLK, PW)
                found = dot(lhs, z, NT)
                bz_ref[s, :, first + i, :] = found[0 : 2 * H, 0:BLK]
                bz_ref[s, :, first + i + 1, :] = found[2 * H :, BLK:]

            for c in range(STEP // CHUNK):
                bz_copy(s, k * (STEP // CHUNK) + c).start()
            return carry

        lax.fori_loop(0, BLK // STEP, some, 0)
    for copy in stores:
        copy.wait()
    for s in range(CAP):
        for k in range(BLK // CHUNK):
            bz_copy(s, k).wait()


def logit_kernel(codes_ref, keys_hbm, qf_hbm, df_hbm, e_hbm, gam_hbm, bz_hbm, mine_hbm, logit_hbm, da_hbm, stat_hbm,
                 keys_ref, qf_ref, df_ref, e_ref, gam_ref, mine_ref, bz_ref, logit_ref, da_ref, ins, outs):
    places = [slot_of(codes_ref, s) for s in range(CAP)]
    small = fetch((e_hbm, gam_hbm), (e_ref, gam_ref), ins)
    loads = []
    for s, (_, qb, kb) in enumerate(places):
        loads.append(fetch(
            (keys_hbm.at[rows_of(kb)], qf_hbm.at[rows_of(qb)], df_hbm.at[rows_of(qb)], bz_hbm.at[s]),
            (keys_ref.at[s], qf_ref.at[s], df_ref.at[s], bz_ref.at[s]), ins, 2 + 4 * s,
        ))
    stores = []
    for copy in small:
        copy.wait()
    e = e_ref[...]
    lane = lax.broadcasted_iota(jnp.int32, (BLK, BLK), 1)
    stats = []
    for s in range(CAP):
        listed, qb, kb = places[s]
        for copy in loads[s][:3]:
            copy.wait()
        kf = keys_ref[s, :, 0:FG]
        vf = keys_ref[s, :, FG:]
        qf = qf_ref[s]
        df = df_ref[s]
        qhi, qlo = split2(jnp.square(qf.astype(F32)))
        khi, klo = split2(jnp.square(kf.astype(F32)))
        ep = e[16:32]
        qn = dot(qhi, ep, NT) + dot(qlo, ep, NT)
        kn = dot(ep, khi, NT) + dot(ep, klo, NT)
        held = jnp.zeros((BLK, BLK), F32)
        loads[s][3].wait()
        for h in range(0, H, 2):
            at = slice(h // GH * GF, h // GH * GF + GF)
            kg = kf[:, at]
            vg = vf[:, at]
            qg = qf[:, at]
            das = dot(df[:, at], jnp.concatenate([vg * e[32 + h : 33 + h, at], vg * e[33 + h : 34 + h, at]], axis=0), NT)
            for n in range(2):
                u = h + n
                both = dot(qg, jnp.concatenate([kg * e[u : u + 1, at], kg * e[16 + u : 17 + u, at]], axis=0), NT)
                dist = qn[:, u : u + 1] + kn[u : u + 1, :] - 2.0 * both[:, BLK:]
                logit = (WL * SC) * both[:, :BLK] + WL * bz_ref[s, u] - (0.5 * WL * WC) * gam_ref[u : u + 1] * dist
                da = bz_ref[s, H + u] + das[:, n * BLK : (n + 1) * BLK]
                logit_ref[s, u] = logit
                da_ref[s, u] = da
                top = jnp.max(logit, axis=1, keepdims=True)
                p = jnp.exp(logit - top)
                total = jnp.sum(p, axis=1, keepdims=True)
                mean = jnp.sum(p * da, axis=1, keepdims=True) / total
                held = jnp.where(lane == u, top + jnp.log(total), held)
                held = jnp.where(lane == 16 + u, mean, held)
            if h % 4 == 2:
                some = pl.ds(h - 2, 4)
                for n, (ref, hbm) in enumerate(((logit_ref, logit_hbm), (da_ref, da_hbm))):
                    at = (2 * s + n) * (H // 4) + h // 4
                    stores.append(pltpu.make_async_copy(ref.at[s, some], hbm.at[s, some], outs.at[at]))
                    stores[-1].start()
        stats.append((listed, qb, jnp.transpose(held)))
    for b in range(2):
        lse = []
        for listed, qb, held in stats:
            lse.append(jnp.where(jnp.logical_and(listed, qb == b), held[0:16], NEG))
        top = jnp.maximum(lse[0], lse[1])
        w0 = jnp.exp(lse[0] - top)
        w1 = jnp.exp(lse[1] - top)
        total = w0 + w1
        merged = jnp.concatenate(
            [top + jnp.log(total), (w0 * stats[0][2][16:32] + w1 * stats[1][2][16:32]) / total], axis=0
        )
        mine_ref[:, b * BLK : (b + 1) * BLK] = merged
    stores.extend(fetch([mine_ref] * (N_COL + 1), [mine_hbm] + [stat_hbm.at[d] for d in range(N_COL)], ins))
    for copy in stores:
        copy.wait()


def out_kernel(codes_ref, pair_ref, logit_hbm, keys_hbm, stat_hbm, e_hbm, o_hbm, held, p_ref, nz_ref, cat_ref, bd_ref, sems,
               logit_ref, keys_ref, stat_ref, e_ref, o_ref, ins):
    places = [slot_of(codes_ref, s) for s in range(CAP)]
    loads = fetch((stat_hbm, e_hbm), (stat_ref, e_ref), ins)
    for s, (_, _, kb) in enumerate(places):
        loads.extend(fetch((logit_hbm.at[s], keys_hbm.at[rows_of(kb), pl.ds(FG, FG)]), (logit_ref.at[s], keys_ref.at[s]), ins, 2 + 2 * s))
    for k in range(CHUNKS):
        pair_copy(pair_ref, held, sems, k).start()
    loads[0].wait()
    loads[1].wait()
    o_ref[...] = jnp.zeros_like(o_ref)
    for s in range(CAP):
        listed, qb, kb = places[s]
        lse = jnp.transpose(jnp.concatenate([stat_ref[:, rows_of(qb)], jnp.zeros((96, BLK), F32)], axis=0))
        lse = jnp.where(listed, lse, -NEG)
        loads[2 + 2 * s].wait()
        loads[3 + 2 * s].wait()
        vf = keys_ref[s]
        for h in range(H):
            at = slice(h // GH * GF, h // GH * GF + GF)
            p = jnp.exp(logit_ref[s, h] - lse[:, h : h + 1])
            p_ref[h] = p
            cat_ref[:, h * BLK : (h + 1) * BLK] = p.astype(BF16)
            bd_ref[h * BLK : (h + 1) * BLK, :] = vf[:, at] * e_ref[32 + h : 33 + h, at]
        for g in range(G):
            at = slice(g * GJ, (g + 1) * GJ)
            o_ref[rows_of(qb), g * GF : (g + 1) * GF] += dot(cat_ref[:, at], bd_ref[at, :])

        def some(k, carry, s=s):
            for c in range(STEP // CHUNK):
                rows = pl.ds(pl.multiple_of(s * BLK + k * STEP + c * CHUNK, CHUNK), CHUNK)
                at = s * (BLK // CHUNK) + k * (STEP // CHUNK) + c
                pltpu.make_async_copy(pair_ref.at[rows], held.at[rows], sems.at[at]).wait()
            first = k * STEP
            zero = jnp.zeros((H, BLK), F32)
            for i in range(0, STEP, 2):
                w = jnp.concatenate(
                    [
                        jnp.concatenate([p_ref[:, first + i, :], zero], axis=1),
                        jnp.concatenate([zero, p_ref[:, first + i + 1, :]], axis=1),
                    ],
                    axis=0,
                ).astype(BF16)
                found = dot(w, held[pl.ds(s * BLK + first + i, 2)].reshape(2 * BLK, PW))
                nz_ref[:, first + i, :] = found[0:H]
                nz_ref[:, first + i + 1, :] = found[H:]
            return carry

        lax.fori_loop(0, BLK // STEP, some, 0)
        for h in range(H):
            o_ref[rows_of(qb), FG + h * PW : FG + (h + 1) * PW] += nz_ref[h]
    (copy,) = fetch((o_ref,), (o_hbm,), ins)
    copy.wait()


def back_kernel(codes_ref, stat_hbm, stats_hbm, keys_hbm, qf_hbm, df_hbm, e_hbm, gam_hbm, logit_hbm, da_hbm, o_hbm,
                whole_hbm, keep_hbm, kg_hbm, send_hbm,
                mine_ref, all_ref, keys_ref, qf_ref, df_ref, e_ref, gam_ref, logit_ref, da_ref, o_ref, ins,
                whole_ref, keep_ref, kg_ref, send_ref, sems, kg_acc, gcat, gstk, astk, kbd, qbd, dbd, ebd, dq_acc, msg):
    places = [slot_of(codes_ref, s) for s in range(CAP)]
    small = fetch((stat_hbm, stats_hbm, e_hbm, gam_hbm), (mine_ref, all_ref, e_ref, gam_ref), ins)
    loads = []
    for s, (_, qb, kb) in enumerate(places):
        loads.append(fetch(
            (logit_hbm.at[s], da_hbm.at[s], keys_hbm.at[rows_of(kb), pl.ds(0, FG)], qf_hbm.at[rows_of(qb)], df_hbm.at[rows_of(qb)]),
            (logit_ref.at[s], da_ref.at[s], keys_ref.at[s], qf_ref.at[s], df_ref.at[s]), ins, 10 + 5 * s,
        ))
    (o_copy,) = fetch((o_hbm,), (o_ref,), ins, 20)
    for copy in small:
        copy.wait()
    held = [all_ref[d] for d in range(N_COL)]
    top = held[0][0:16]
    for d in range(1, N_COL):
        top = jnp.maximum(top, held[d][0:16])
    total = jnp.zeros((16, QR), F32)
    mean = jnp.zeros((16, QR), F32)
    for d in range(N_COL):
        w = jnp.exp(held[d][0:16] - top)
        total = total + w
        mean = mean + w * held[d][16:32]
    lse = top + jnp.log(total)
    delta = mean / total
    alpha = jnp.exp(mine_ref[0:16] - lse)
    whole_t = jnp.concatenate([lse, delta, alpha, jnp.zeros((80, QR), F32)], axis=0)
    whole = jnp.transpose(whole_t)
    whole_ref[...] = whole
    e = e_ref[32:48]
    gam_f = jnp.sum(e.astype(F32) * gam_ref[:, 0:1], axis=0, keepdims=True)
    point = jnp.sum(e_ref[16:32].astype(F32), axis=0, keepdims=True)
    scalar = jnp.sum(e_ref[0:16].astype(F32), axis=0, keepdims=True)
    fa = WC * gam_f * point + SC * scalar
    fb = -WC * gam_f * point
    kg_acc[...] = jnp.zeros_like(kg_acc)
    dq_acc[...] = jnp.zeros_like(dq_acc)
    for h in range(H):
        at = slice(h // GH * GF, h // GH * GF + GF)
        ebd[h * BLK : (h + 1) * BLK, :] = jnp.broadcast_to(e[h : h + 1, at], (BLK, GF))
    for s in range(CAP):
        listed, qb, kb = places[s]
        for copy in loads[s]:
            copy.wait()
        stat = jnp.where(qb == 0, whole[0:BLK], whole[BLK:])
        lse_s = jnp.where(listed, stat, -NEG)
        kf = keys_ref[s]
        qf = qf_ref[s]
        df = df_ref[s]
        for h in range(H):
            at = slice(h // GH * GF, h // GH * GF + GF)
            block = slice(h * BLK, (h + 1) * BLK)
            a = jnp.exp(logit_ref[s, h] - lse_s[:, h : h + 1])
            g = WL * a * (da_ref[s, h] - stat[:, 16 + h : 17 + h])
            gr = g.astype(BF16)
            gcat[:, block] = gr
            gstk[block, :] = gr
            astk[block, :] = a.astype(BF16)
            eh = e[h : h + 1, at]
            kbd[block, :] = kf[:, at] * eh
            qbd[block, :] = qf[:, at] * eh
            dbd[block, :] = df[:, at] * eh
        for g in range(G):
            at = slice(g * GF, (g + 1) * GF)
            block = slice(g * GJ, (g + 1) * GJ)
            dq_raw = dot(gcat[:, block], kbd[block, :])
            row_sum = dot(gcat[:, block], ebd[block, :])
            dq_acc[rows_of(qb), at] += fa[:, at] * dq_raw + fb[:, at] * row_sum * qf[:, at].astype(F32)
            dk_raw = dot(gstk[block, :], qbd[block, :], TN)
            col_sum = dot(gstk[block, :], ebd[block, :], TN)
            kg_acc[rows_of(kb), at] += fa[:, at] * dk_raw + fb[:, at] * col_sum * kf[:, at].astype(F32)
            kg_acc[rows_of(kb), FG + g * GF : FG + (g + 1) * GF] += dot(astk[block, :], dbd[block, :], TN)
    kg_ref[...] = kg_acc[...].astype(BF16)
    kg_copy = pltpu.make_async_copy(kg_ref, kg_hbm, sems.at[0])
    kg_copy.start()
    o_copy.wait()
    ahi, alo = split2(whole[:, 32:48])
    msg[:, 0:FG] = (o_ref[:, 0:FG] * (dot(ahi, e) + dot(alo, e))).astype(BF16)
    for h in range(H):
        at = slice(FG + h * PW, FG + (h + 1) * PW)
        msg[:, at] = (o_ref[:, at] * whole[:, 32 + h : 33 + h]).astype(BF16)
    msg[:, 2048:] = dq_acc[...].astype(BF16)
    core = lax.axis_index("col") % 2
    for x in range(4):
        keep_ref[x] = msg[pl.ds(pl.multiple_of((2 * x + core) * OWN, OWN), OWN), :]
        send_ref[x] = msg[pl.ds(pl.multiple_of((2 * x + 1 - core) * OWN, OWN), OWN), :]
    copies = fetch((send_ref, keep_ref, whole_ref), (send_hbm, keep_hbm, whole_hbm), sems, 1)
    for copy in [kg_copy] + copies:
        copy.wait()


def fold_kernel(keep_ref, got_ref, own_ref, one_ref, two_ref, three_ref):
    x = lax.axis_index("col") // 2
    for k, ref in enumerate((own_ref, one_ref, two_ref, three_ref)):
        at = (x + k) % 4
        ref[...] = (keep_ref[at].astype(F32) + got_ref[at].astype(F32)).astype(BF16)


def pair_out_kernel(codes_ref, whole_hbm, logit_hbm, da_hbm, dzp_hbm, out_ref, held, ga, sems, logit_ref, da_ref, dzp_ref, whole_ref, ins):
    (whole_copy,) = fetch((whole_hbm,), (whole_ref,), ins, 2 * CAP + 1)
    loads = []
    for s in range(CAP):
        loads.append(pltpu.make_async_copy(logit_hbm.at[s], logit_ref.at[s], ins.at[2 * s]))
        loads.append(pltpu.make_async_copy(da_hbm.at[s], da_ref.at[s], ins.at[2 * s + 1]))
    loads.insert(2, pltpu.make_async_copy(dzp_hbm, dzp_ref, ins.at[2 * CAP]))
    for copy in loads:
        copy.start()
    whole_copy.wait()
    for s in range(CAP):
        listed, qb, _ = slot_of(codes_ref, s)
        stat = whole_ref[rows_of(qb), :]
        lse_s = jnp.where(listed, stat, -NEG)
        for copy in loads[0:2] if s == 0 else loads[3:5]:
            copy.wait()
        for h in range(H):
            a = jnp.exp(logit_ref[s, h] - lse_s[:, h : h + 1])
            ga[h] = WL * a * (da_ref[s, h] - stat[:, 16 + h : 17 + h])
            ga[H + h] = a
        if s == 0:
            loads[2].wait()

        def some(k, carry, s=s, qb=qb):
            first = k * STEP
            zero = jnp.zeros((2 * H, PW), BF16)
            for i in range(0, STEP, 2):
                lhs = jnp.concatenate([ga[:, first + i, :], ga[:, first + i + 1, :]], axis=0).astype(BF16)
                one = dzp_ref[qb * BLK + first + i].astype(BF16)
                two = dzp_ref[qb * BLK + first + i + 1].astype(BF16)
                rhs = jnp.concatenate(
                    [jnp.concatenate([one, zero], axis=1), jnp.concatenate([zero, two], axis=1)], axis=0
                )
                found = dot(lhs, rhs, TN).astype(BF16)
                held[s * BLK + first + i] = found[:, :PW]
                held[s * BLK + first + i + 1] = found[:, PW:]

                if i % CHUNK == CHUNK - 2:
                    rows = pl.ds(pl.multiple_of(s * BLK + k * STEP + i + 2 - CHUNK, CHUNK), CHUNK)
                    at = s * (BLK // CHUNK) + k * (STEP // CHUNK) + i // CHUNK
                    pltpu.make_async_copy(held.at[rows], out_ref.at[rows], sems.at[at]).start()
            return carry

        lax.fori_loop(0, BLK // STEP, some, 0)
    for k in range(CHUNKS):
        pair_copy(held, out_ref, sems, k).wait()


def final_kernel(kg_ref, own_ref, one_ref, two_ref, three_ref, frame_q_ref, frame_k_ref, ow_hbm, up_ref, gq_ref, gk_ref, ow_ref, sems):
    (ow_copy,) = fetch((ow_hbm,), (ow_ref,), sems)
    total = kg_ref[0].astype(F32)
    for d in range(1, N_ROW):
        total = total + kg_ref[d].astype(F32)
    fk = frame_k_ref[...]
    fq = frame_q_ref[pl.ds(pl.multiple_of(lax.axis_index("col") * OWN, OWN), OWN), :]
    dk, dgk = ungrouped(total[:, :FG])
    dv, dgv = ungrouped(total[:, FG:])
    gk_ref[...] = jnp.concatenate(
        [dk, dv] + rotate_back(dgk, fk, False) + rotate_back(dgv, fk, False), axis=1
    ).astype(BF16)
    msg = (own_ref[...].astype(F32) + one_ref[...].astype(F32)) + (two_ref[...].astype(F32) + three_ref[...].astype(F32))
    scalar, parts = ungrouped(msg[:, :FG])
    head = jnp.concatenate([scalar] + rotate_back(parts, fq, True), axis=1).astype(BF16)
    tail = msg[:, FG:2048].astype(BF16)
    ow_copy.wait()
    up_ref[...] = (dot(head, ow_ref[0:F]) + dot(tail, ow_ref[F:])).astype(BF16)
    dq, dgq = ungrouped(msg[:, 2048:])
    gq_ref[...] = jnp.concatenate([dq] + rotate_back(dgq, fq, False), axis=1).astype(BF16)


SMEM = pl.BlockSpec(memory_space=pltpu.SMEM)
FULL = pl.BlockSpec(memory_space=pltpu.VMEM)
HBM = pl.BlockSpec(memory_space=pltpu.HBM)
DMA = pltpu.SemaphoreType.DMA


def call(kernel, name, ins, outs, scratch, mb, flops=0, nbytes=0):
    return pl.pallas_call(
        kernel,
        name=name,
        in_specs=ins,
        out_specs=[spec for _, spec in outs],
        out_shape=[shape for shape, _ in outs],
        scratch_shapes=scratch,
        compiler_params=pltpu.CompilerParams(vmem_limit_bytes=56 * MB if mb > 12 else mb * MB),
        cost_estimate=pl.CostEstimate(flops=flops, bytes_accessed=nbytes, transcendentals=0),
    )


def near(dims, kind):
    return jax.ShapeDtypeStruct(dims, kind), FULL


def far(dims, kind):
    return jax.ShapeDtypeStruct(dims, kind), HBM


def free(dims, kind):
    return jax.ShapeDtypeStruct(dims, kind), FULL


def on_device(queries, keys, frame_table, frame_index, pair_list, pair, pair_weight, point_weight, out_weight, cotangent):
    codes = pair_list.reshape(CAP)
    tiles = pair.reshape(CAP * BLK, BLK, PW)
    e = jnp.asarray(head_rows(), BF16)
    index = frame_index.reshape(1, NRES)
    sems = DMA((CHUNKS,))
    held = pltpu.VMEM((CAP * BLK, BLK, PW), BF16)
    table = pltpu.VMEM((12, NRES), F32)
    where = pltpu.VMEM((1, NRES), jnp.int32)
    planes = (CAP, H, BLK, BLK)

    key_wire, frame_k = call(
        key_kernel, "keys", [HBM] * 3, [far((N_ROW, OWN, 2 * FG), BF16), near((OWN, BLK), F32)],
        [pltpu.VMEM((BLK, BLK), F32), pltpu.VMEM((OWN, 2 * F), BF16), table, where, pltpu.VMEM((OWN, 2 * FG), BF16),
         DMA((3 + N_ROW,))], 56,
    )(keys, frame_table, index)
    key_all = lax.all_to_all(key_wire, "row", split_axis=0, concat_axis=0).reshape(KR, 2 * FG)

    half = pltpu.VMEM((CAP, BLK, FG), BF16)
    marks = pltpu.VMEM((48, FG), BF16)
    gammas = pltpu.VMEM((16, BLK), F32)
    rows = pltpu.VMEM((QR, FG), BF16)
    plane_buf = pltpu.VMEM(planes, F32)
    dzp_buf = pltpu.VMEM((QR, 2 * H, PW), F32)
    bz_buf = pltpu.VMEM((CAP, 2 * H, BLK, BLK), F32)
    qf, df, frame_q, gam, dzp, bz = call(
        prep_kernel, "prep", [SMEM] + [HBM] * 8,
        [far((QR, FG), BF16), far((QR, FG), BF16), far((QR, BLK), F32), far((16, BLK), F32),
         far((QR, 2 * H, PW), F32), far((CAP, 2 * H, BLK, BLK), F32)],
        [held, sems, table, where, pltpu.VMEM((1, H), F32), pltpu.VMEM((F, QR), BF16), pltpu.VMEM((QR, SW), BF16),
         pltpu.VMEM((2016, SW), BF16), pltpu.VMEM((H, PW), BF16), DMA((7,)),
         rows, rows, pltpu.VMEM((QR, BLK), F32), gammas, dzp_buf, bz_buf, DMA((CHUNKS + 5,))],
        56, flops=3_000_000_000, nbytes=30_000_000,
    )(codes, queries.T, pair_weight.T, point_weight.reshape(1, H), frame_table, index, cotangent, out_weight, tiles)

    mine, logit, da, stat = call(
        logit_kernel, "logit", [SMEM] + [HBM] * 6, [far((32, QR), F32), far(planes, F32), far(planes, F32), far((N_COL, 32, QR), F32)],
        [pltpu.VMEM((CAP, BLK, 2 * FG), BF16), half, half, marks, gammas, pltpu.VMEM((32, QR), F32), bz_buf, plane_buf,
         plane_buf, DMA((10,)), DMA((H,))], 56,
    )(codes, key_all, qf, df, e, gam, bz)

    stat_all = lax.all_to_all(stat, "col", split_axis=0, concat_axis=0)

    (out,) = call(
        out_kernel, "local_out", [SMEM] + [HBM] * 5, [far((QR, 2048), F32)],
        [held, pltpu.VMEM((H, BLK, BLK), F32), pltpu.VMEM((H, BLK, PW), F32), pltpu.VMEM((BLK, HJ), BF16),
         pltpu.VMEM((HJ, GF), BF16), sems, plane_buf, half, pltpu.VMEM((32, QR), F32), marks,
         pltpu.VMEM((QR, 2048), F32), DMA((6,))], 56, flops=2_000_000_000, nbytes=20_000_000,
    )(codes, tiles, logit, key_all, mine, e)

    whole, keep, kg, send = call(
        back_kernel, "back", [SMEM] + [HBM] * 10,
        [far((QR, BLK), F32), far((4, OWN, 2560), BF16), far((KR, 2 * FG), BF16), far((4, OWN, 2560), BF16)],
        [pltpu.VMEM((32, QR), F32), pltpu.VMEM((N_COL, 32, QR), F32), half, half, half, marks, gammas, plane_buf, plane_buf,
         pltpu.VMEM((QR, 2048), F32), DMA((21,)),
         pltpu.VMEM((QR, BLK), F32), pltpu.VMEM((4, OWN, 2560), BF16), pltpu.VMEM((KR, 2 * FG), BF16),
         pltpu.VMEM((4, OWN, 2560), BF16), DMA((4,)),
         pltpu.VMEM((KR, 2 * FG), F32), pltpu.VMEM((BLK, HJ), BF16), pltpu.VMEM((HJ, BLK), BF16),
         pltpu.VMEM((HJ, BLK), BF16), pltpu.VMEM((HJ, GF), BF16), pltpu.VMEM((HJ, GF), BF16),
         pltpu.VMEM((HJ, GF), BF16), pltpu.VMEM((HJ, GF), BF16), pltpu.VMEM((QR, FG), F32),
         pltpu.VMEM((QR, 2560), BF16)], 56,
    )(codes, mine, stat_all, key_all, qf, df, e, gam, logit, da, out)

    kg_all = lax.all_to_all(kg.reshape(N_ROW, OWN, 2 * FG), "row", split_axis=0, concat_axis=0)
    got = lax.ppermute(send, "col", [(d, d ^ 1) for d in range(N_COL)])
    own, *away = call(
        fold_kernel, "fold", [FULL] * 2, [near((OWN, 2560), BF16)] + [free((OWN, 2560), BF16)] * 3, [], 4
    )(keep, got)
    came = [
        lax.ppermute(part, "col", [(d, (d + 2 * k) % N_COL) for d in range(N_COL)])
        for k, part in enumerate(away, 1)
    ]

    (grad_tiles,) = call(
        pair_out_kernel, "pair_out", [SMEM] + [HBM] * 4, [far((CAP * BLK, BLK, PW), BF16)],
        [held, pltpu.VMEM((2 * H, BLK, BLK), F32), sems, plane_buf, plane_buf, dzp_buf,
         pltpu.VMEM((QR, BLK), F32), DMA((2 * CAP + 2,))], 56, flops=4_000_000_000, nbytes=30_000_000,
    )(codes, whole, logit, da, dzp)

    update, grad_queries, grad_keys = call(
        final_kernel, "final", [FULL] * 7 + [HBM],
        [free((OWN, SW), BF16), free((OWN, F), BF16), free((OWN, 2 * F), BF16)],
        [pltpu.VMEM((2016, SW), BF16), DMA((1,))], 12,
    )(kg_all, own, *came, frame_q, frame_k, out_weight)
    return update, grad_queries, grad_keys, grad_tiles.reshape(pair.shape)


def solution(mesh):
    in_specs = (
        P("row", None),
        P(("col", "row"), None),
        P(),
        P(),
        P("row", "col", None),
        P("row", "col", None, None, None, None),
        P(),
        P(),
        P(),
        P("row", None),
    )
    out_specs = (
        P(("row", "col"), None),
        P(("row", "col"), None),
        P(("col", "row"), None),
        P("row", "col", None, None, None, None),
    )
    return jax.shard_map(on_device, mesh=mesh, in_specs=in_specs, out_specs=out_specs, check_vma=False)
```

```python
import functools
import math

import jax
import jax.numpy as jnp
import numpy as np
from jax import lax
from jax.experimental import pallas as pl
from jax.experimental.pallas import tpu as pltpu
from jax.sharding import PartitionSpec as P

H = 12
C = 16
PV = 8
PW = 128
BLK = 128
SW = 384
QR = 256
KR = 512
NRES = 4096
KEYB = 4
CAP = 2
F = 480
WS = 192
WP = 288
HJ = H * BLK
GJ = 6 * BLK
N_ROW = 16
N_COL = 8
OWN = 32
EMPTY = 8
NEG = -1e30
SC = 1.0 / math.sqrt(C)
WC = math.sqrt(2.0 / 72.0)
WL = math.sqrt(1.0 / 3.0)
F32 = jnp.float32
BF16 = jnp.bfloat16
MB = 1024 * 1024
G = 2
GH = 6
GF = 256
FG = G * GF
CHUNK = 32
STEP = 64

NN = (((1,), (0,)), ((), ()))
NT = (((1,), (1,)), ((), ()))
TN = (((0,), (0,)), ((), ()))


def head_rows():
    f = np.arange(FG)
    group, at = f // GF, f % GF
    head = np.where(at < 96, at // C, ((at - 96) % 48) // PV) + GH * group
    mine = (head[None, :] == np.arange(16)[:, None]) & (at < 240)[None, :]
    scalar, point = mine & (at < 96)[None, :], mine & (at >= 96)[None, :]
    return np.concatenate([scalar, point, mine], axis=0).astype(np.float32)


def dot(a, b, dims=NN):
    return lax.dot_general(a, b, dims, preferred_element_type=F32)


def split3(x):
    hi = x.astype(BF16)
    rest = x - hi.astype(F32)
    mid = rest.astype(BF16)
    lo = (rest - mid.astype(F32)).astype(BF16)
    return hi, mid, lo


def split2(x):
    hi = x.astype(BF16)
    return hi, (x - hi.astype(F32)).astype(BF16)


def rotate(parts, frame, shift):
    out = []
    for a in range(3):
        y = sum(frame[:, 3 * a + b : 3 * a + b + 1] * parts[b] for b in range(3))
        if shift:
            y = y + frame[:, 9 + a : 10 + a]
        out.append(y)
    return out


def rotate_back(parts, frame, shift):
    if shift:
        parts = [parts[a] - frame[:, 9 + a : 10 + a] for a in range(3)]
    return [sum(frame[:, 3 * a + b : 3 * a + b + 1] * parts[a] for a in range(3)) for b in range(3)]


def components(x):
    return [x[:, 96 * b : 96 * b + 96] for b in range(3)]


def grouped(scalar, parts):
    pad = jnp.zeros((scalar.shape[0], 16), F32)
    pieces = []
    for g in range(G):
        pieces.append(scalar[:, 96 * g : 96 * g + 96])
        pieces.extend(part[:, 48 * g : 48 * g + 48] for part in parts)
        pieces.append(pad)
    return jnp.concatenate(pieces, axis=1).astype(BF16)


def ungrouped(x):
    scalar = jnp.concatenate([x[:, GF * g : GF * g + 96] for g in range(G)], axis=1)
    parts = []
    for a in range(3):
        first = 96 + 48 * a
        parts.append(jnp.concatenate([x[:, GF * g + first : GF * g + first + 48] for g in range(G)], axis=1))
    return scalar, parts


def slot_of(codes_ref, s):
    code = codes_ref[s]
    listed = code < EMPTY
    safe = jnp.where(listed, code, 0)
    return listed, safe // KEYB, safe % KEYB


def rows_of(block):
    return pl.ds(pl.multiple_of(block * BLK, BLK), BLK)


def fetch(refs, held, sems, first=0):
    copies = [pltpu.make_async_copy(ref, buf, sems.at[first + n]) for n, (ref, buf) in enumerate(zip(refs, held))]
    for copy in copies:
        copy.start()
    return copies


def look_up(table_ref, ids):
    count = ids.shape[1]
    found = jnp.zeros((48, count), F32)
    step = 512
    pad = jnp.zeros((4, step), F32)
    for first in range(0, NRES, step):
        table = jnp.concatenate([table_ref[:, first : first + step], pad], axis=0)
        table = jnp.concatenate(split3(table), axis=0)
        at = lax.broadcasted_iota(jnp.int32, (step, count), 0) + first
        found = found + dot(table, jnp.where(at == ids, 1.0, 0.0).astype(BF16))
    return found[0:16] + found[16:32] + found[32:48]


def key_kernel(keys_hbm, table_hbm, index_hbm, wire_hbm, frame_ref, held_ref, keys_ref, table_ref, index_ref, wire_ref, sems):
    copies = fetch((keys_hbm, table_hbm, index_hbm), (keys_ref, table_ref, index_ref), sems)
    for copy in copies:
        copy.wait()
    at = lax.axis_index("col") * N_ROW + lax.axis_index("row")
    window = at // 4
    ids = index_ref[:, pl.ds(pl.multiple_of(window * BLK, BLK), BLK)]
    held_ref[...] = jnp.transpose(jnp.concatenate([look_up(table_ref, ids), jnp.zeros((112, BLK), F32)], axis=0))
    frame = held_ref[pl.ds(pl.multiple_of((at % 4) * OWN, OWN), OWN), :]
    frame_ref[...] = frame
    keys = keys_ref[...].astype(F32)
    gk = rotate(components(keys[:, 2 * WS : 2 * WS + WP]), frame, True)
    gv = rotate(components(keys[:, 2 * WS + WP :]), frame, True)
    wire = jnp.concatenate([grouped(keys[:, :WS], gk), grouped(keys[:, WS : 2 * WS], gv)], axis=1)
    for d in range(N_ROW):
        wire_ref[d] = wire
    copies = [pltpu.make_async_copy(wire_ref.at[pl.ds(4 * d, 4)], wire_hbm.at[pl.ds(4 * d, 4)], sems.at[3 + d]) for d in range(4)]
    for copy in copies:
        copy.start()
    for copy in copies:
        copy.wait()


def pair_copy(pair_ref, held, sems, k):
    rows = pl.ds(k * CHUNK, CHUNK)
    return pltpu.make_async_copy(pair_ref.at[rows], held.at[rows], sems.at[k])


CHUNKS = CAP * BLK // CHUNK


def prep_kernel(codes_ref, q_hbm, pw_hbm, gam_hbm, table_hbm, index_hbm, cot_hbm, ow_hbm, pair_ref,
                qf_hbm, df_hbm, frame_hbm, gamma_hbm, dzp_hbm, bz_hbm,
                held, sems, table_ref, index_ref, gam_ref, q_ref, cot_ref, ow_ref, pw_ref, more,
                qf_ref, df_ref, frame_ref, gamma_ref, dzp_ref, bz_ref, outs):
    loads = fetch((table_hbm, index_hbm, gam_hbm, q_hbm, cot_hbm, ow_hbm, pw_hbm),
                  (table_ref, index_ref, gam_ref, q_ref, cot_ref, ow_ref, pw_ref), more)
    for k in range(CHUNKS):
        pair_copy(pair_ref, held, sems, k).start()
    row = lax.axis_index("row")
    for copy in loads[:3]:
        copy.wait()
    frame_t = look_up(table_ref, index_ref[:, pl.ds(pl.multiple_of(row * QR, QR), QR)])
    frame = jnp.transpose(jnp.concatenate([frame_t, jnp.zeros((112, QR), F32)], axis=0))
    frame_ref[...] = frame
    raw = gam_ref[...]
    soft = jnp.maximum(raw, 0.0) + jnp.log(1.0 + jnp.exp(-jnp.abs(raw)))
    diag = lax.broadcasted_iota(jnp.int32, (16, H), 0) == lax.broadcasted_iota(jnp.int32, (16, H), 1)
    gamma_ref[...] = jnp.broadcast_to(jnp.sum(jnp.where(diag, soft, 0.0), axis=1, keepdims=True), (16, BLK))
    for copy in loads[3:]:
        copy.wait()
    q = jnp.transpose(q_ref[...].astype(F32))
    qf_ref[...] = grouped(q[:, :WS], rotate(components(q[:, WS:]), frame, True))
    cot = cot_ref[...]
    head = dot(cot, ow_ref[0:F], NT).astype(BF16).astype(F32)
    df_ref[...] = grouped(head[:, :WS], rotate(components(head[:, WS:]), frame, False))
    tail = dot(cot, ow_ref[F:], NT).astype(BF16).astype(F32)
    pwt = pw_ref[...].astype(F32)
    for h in range(H):
        dzp_ref[:, h, :] = jnp.broadcast_to(pwt[h : h + 1], (QR, PW))
        dzp_ref[:, H + h, :] = tail[:, h * PW : (h + 1) * PW]
    stores = fetch((qf_ref, df_ref, frame_ref, gamma_ref, dzp_ref), (qf_hbm, df_hbm, frame_hbm, gamma_hbm, dzp_hbm), outs, CHUNKS)

    def bz_copy(s, k):
        rows = pl.ds(k * CHUNK, CHUNK)
        return pltpu.make_async_copy(bz_ref.at[s, :, rows], bz_hbm.at[s, :, rows], outs.at[s * (BLK // CHUNK) + k])

    for s in range(CAP):
        _, qb, _ = slot_of(codes_ref, s)

        def some(k, carry, s=s, qb=qb):
            for c in range(STEP // CHUNK):
                rows = pl.ds(pl.multiple_of(s * BLK + k * STEP + c * CHUNK, CHUNK), CHUNK)
                at = s * (BLK // CHUNK) + k * (STEP // CHUNK) + c
                pltpu.make_async_copy(pair_ref.at[rows], held.at[rows], sems.at[at]).wait()
            first = k * STEP
            for i in range(0, STEP, 2):
                lhs = dzp_ref[pl.ds(qb * BLK + first + i, 2)].reshape(4 * H, PW).astype(BF16)
                z = held[pl.ds(s * BLK + first + i, 2)].reshape(2 * BLK, PW)
                found = dot(lhs, z, NT)
                bz_ref[s, :, first + i, :] = found[0 : 2 * H, 0:BLK]
                bz_ref[s, :, first + i + 1, :] = found[2 * H :, BLK:]

            for c in range(STEP // CHUNK):
                bz_copy(s, k * (STEP // CHUNK) + c).start()
            return carry

        lax.fori_loop(0, BLK // STEP, some, 0)
    for copy in stores:
        copy.wait()
    for s in range(CAP):
        for k in range(BLK // CHUNK):
            bz_copy(s, k).wait()


def logit_kernel(codes_ref, keys_hbm, qf_hbm, df_hbm, e_hbm, gam_hbm, bz_hbm, mine_hbm, logit_hbm, da_hbm, stat_hbm,
                 keys_ref, qf_ref, df_ref, e_ref, gam_ref, mine_ref, bz_ref, logit_ref, da_ref, ins, outs):
    places = [slot_of(codes_ref, s) for s in range(CAP)]
    small = fetch((e_hbm, gam_hbm), (e_ref, gam_ref), ins)
    loads = []
    for s, (_, qb, kb) in enumerate(places):
        loads.append(fetch(
            (keys_hbm.at[rows_of(kb)], qf_hbm.at[rows_of(qb)], df_hbm.at[rows_of(qb)], bz_hbm.at[s]),
            (keys_ref.at[s], qf_ref.at[s], df_ref.at[s], bz_ref.at[s]), ins, 2 + 4 * s,
        ))
    stores = []
    for copy in small:
        copy.wait()
    e = e_ref[...]
    lane = lax.broadcasted_iota(jnp.int32, (BLK, BLK), 1)
    stats = []
    for s in range(CAP):
        listed, qb, kb = places[s]
        for copy in loads[s][:3]:
            copy.wait()
        kf = keys_ref[s, :, 0:FG]
        vf = keys_ref[s, :, FG:]
        qf = qf_ref[s]
        df = df_ref[s]
        qhi, qlo = split2(jnp.square(qf.astype(F32)))
        khi, klo = split2(jnp.square(kf.astype(F32)))
        ep = e[16:32]
        qn = dot(qhi, ep, NT) + dot(qlo, ep, NT)
        kn = dot(ep, khi, NT) + dot(ep, klo, NT)
        held = jnp.zeros((BLK, BLK), F32)
        loads[s][3].wait()
        for h in range(0, H, 2):
            at = slice(h // GH * GF, h // GH * GF + GF)
            kg = kf[:, at]
            vg = vf[:, at]
            qg = qf[:, at]
            das = dot(df[:, at], jnp.concatenate([vg * e[32 + h : 33 + h, at], vg * e[33 + h : 34 + h, at]], axis=0), NT)
            for n in range(2):
                u = h + n
                both = dot(qg, jnp.concatenate([kg * e[u : u + 1, at], kg * e[16 + u : 17 + u, at]], axis=0), NT)
                dist = qn[:, u : u + 1] + kn[u : u + 1, :] - 2.0 * both[:, BLK:]
                logit = (WL * SC) * both[:, :BLK] + WL * bz_ref[s, u] - (0.5 * WL * WC) * gam_ref[u : u + 1] * dist
                da = bz_ref[s, H + u] + das[:, n * BLK : (n + 1) * BLK]
                logit_ref[s, u] = logit
                da_ref[s, u] = da
                top = jnp.max(logit, axis=1, keepdims=True)
                p = jnp.exp(logit - top)
                total = jnp.sum(p, axis=1, keepdims=True)
                mean = jnp.sum(p * da, axis=1, keepdims=True) / total
                held = jnp.where(lane == u, top + jnp.log(total), held)
                held = jnp.where(lane == 16 + u, mean, held)
            if h % 4 == 2:
                some = pl.ds(h - 2, 4)
                for n, (ref, hbm) in enumerate(((logit_ref, logit_hbm), (da_ref, da_hbm))):
                    at = (2 * s + n) * (H // 4) + h // 4
                    stores.append(pltpu.make_async_copy(ref.at[s, some], hbm.at[s, some], outs.at[at]))
                    stores[-1].start()
        stats.append((listed, qb, jnp.transpose(held)))
    for b in range(2):
        lse = []
        for listed, qb, held in stats:
            lse.append(jnp.where(jnp.logical_and(listed, qb == b), held[0:16], NEG))
        top = jnp.maximum(lse[0], lse[1])
        w0 = jnp.exp(lse[0] - top)
        w1 = jnp.exp(lse[1] - top)
        total = w0 + w1
        merged = jnp.concatenate(
            [top + jnp.log(total), (w0 * stats[0][2][16:32] + w1 * stats[1][2][16:32]) / total], axis=0
        )
        mine_ref[:, b * BLK : (b + 1) * BLK] = merged
    stores.extend(fetch([mine_ref] * (N_COL + 1), [mine_hbm] + [stat_hbm.at[d] for d in range(N_COL)], ins))
    for copy in stores:
        copy.wait()


def out_kernel(codes_ref, pair_ref, logit_hbm, keys_hbm, stat_hbm, e_hbm, o_hbm, held, p_ref, nz_ref, cat_ref, bd_ref, sems,
               logit_ref, keys_ref, stat_ref, e_ref, o_ref, low_ref, ins):
    places = [slot_of(codes_ref, s) for s in range(CAP)]
    loads = fetch((stat_hbm, e_hbm), (stat_ref, e_ref), ins)
    for s, (_, _, kb) in enumerate(places):
        loads.extend(fetch((logit_hbm.at[s], keys_hbm.at[rows_of(kb), pl.ds(FG, FG)]), (logit_ref.at[s], keys_ref.at[s]), ins, 2 + 2 * s))
    for k in range(CHUNKS):
        pair_copy(pair_ref, held, sems, k).start()
    loads[0].wait()
    loads[1].wait()
    o_ref[...] = jnp.zeros_like(o_ref)
    for s in range(CAP):
        listed, qb, kb = places[s]
        lse = jnp.transpose(jnp.concatenate([stat_ref[:, rows_of(qb)], jnp.zeros((96, BLK), F32)], axis=0))
        lse = jnp.where(listed, lse, -NEG)
        loads[2 + 2 * s].wait()
        loads[3 + 2 * s].wait()
        vf = keys_ref[s]
        for h in range(H):
            at = slice(h // GH * GF, h // GH * GF + GF)
            p = jnp.exp(logit_ref[s, h] - lse[:, h : h + 1])
            p_ref[h] = p
            cat_ref[:, h * BLK : (h + 1) * BLK] = p.astype(BF16)
            bd_ref[h * BLK : (h + 1) * BLK, :] = vf[:, at] * e_ref[32 + h : 33 + h, at]
        for g in range(G):
            at = slice(g * GJ, (g + 1) * GJ)
            o_ref[rows_of(qb), g * GF : (g + 1) * GF] += dot(cat_ref[:, at], bd_ref[at, :])

        def some(k, carry, s=s):
            for c in range(STEP // CHUNK):
                rows = pl.ds(pl.multiple_of(s * BLK + k * STEP + c * CHUNK, CHUNK), CHUNK)
                at = s * (BLK // CHUNK) + k * (STEP // CHUNK) + c
                pltpu.make_async_copy(pair_ref.at[rows], held.at[rows], sems.at[at]).wait()
            first = k * STEP
            zero = jnp.zeros((H, BLK), F32)
            for i in range(0, STEP, 2):
                w = jnp.concatenate(
                    [
                        jnp.concatenate([p_ref[:, first + i, :], zero], axis=1),
                        jnp.concatenate([zero, p_ref[:, first + i + 1, :]], axis=1),
                    ],
                    axis=0,
                ).astype(BF16)
                found = dot(w, held[pl.ds(s * BLK + first + i, 2)].reshape(2 * BLK, PW))
                nz_ref[:, first + i, :] = found[0:H]
                nz_ref[:, first + i + 1, :] = found[H:]
            return carry

        lax.fori_loop(0, BLK // STEP, some, 0)
        for h in range(H):
            o_ref[rows_of(qb), FG + h * PW : FG + (h + 1) * PW] += nz_ref[h]
    low_ref[...] = o_ref[...].astype(BF16)
    (copy,) = fetch((low_ref,), (o_hbm,), ins)
    copy.wait()


def back_kernel(codes_ref, stat_hbm, stats_hbm, keys_hbm, qf_hbm, df_hbm, e_hbm, gam_hbm, logit_hbm, da_hbm, o_hbm,
                whole_hbm, keep_hbm, kg_hbm, send_hbm,
                mine_ref, all_ref, keys_ref, qf_ref, df_ref, e_ref, gam_ref, logit_ref, da_ref, o_ref, ins,
                whole_ref, keep_ref, kg_ref, send_ref, sems, kg_acc, gcat, gstk, astk, kbd, qbd, dbd, ebd, dq_acc, msg):
    places = [slot_of(codes_ref, s) for s in range(CAP)]
    small = fetch((stat_hbm, stats_hbm, e_hbm, gam_hbm), (mine_ref, all_ref, e_ref, gam_ref), ins)
    loads = []
    for s, (_, qb, kb) in enumerate(places):
        loads.append(fetch(
            (logit_hbm.at[s], da_hbm.at[s], keys_hbm.at[rows_of(kb), pl.ds(0, FG)], qf_hbm.at[rows_of(qb)], df_hbm.at[rows_of(qb)]),
            (logit_ref.at[s], da_ref.at[s], keys_ref.at[s], qf_ref.at[s], df_ref.at[s]), ins, 10 + 5 * s,
        ))
    (o_copy,) = fetch((o_hbm,), (o_ref,), ins, 20)
    for copy in small:
        copy.wait()
    held = [all_ref[d] for d in range(N_COL)]
    top = held[0][0:16]
    for d in range(1, N_COL):
        top = jnp.maximum(top, held[d][0:16])
    total = jnp.zeros((16, QR), F32)
    mean = jnp.zeros((16, QR), F32)
    for d in range(N_COL):
        w = jnp.exp(held[d][0:16] - top)
        total = total + w
        mean = mean + w * held[d][16:32]
    lse = top + jnp.log(total)
    delta = mean / total
    alpha = jnp.exp(mine_ref[0:16] - lse)
    whole_t = jnp.concatenate([lse, delta, alpha, jnp.zeros((80, QR), F32)], axis=0)
    whole = jnp.transpose(whole_t)
    whole_ref[...] = whole
    e = e_ref[32:48]
    gam_f = jnp.sum(e.astype(F32) * gam_ref[:, 0:1], axis=0, keepdims=True)
    point = jnp.sum(e_ref[16:32].astype(F32), axis=0, keepdims=True)
    scalar = jnp.sum(e_ref[0:16].astype(F32), axis=0, keepdims=True)
    fa = WC * gam_f * point + SC * scalar
    fb = -WC * gam_f * point
    kg_acc[...] = jnp.zeros_like(kg_acc)
    dq_acc[...] = jnp.zeros_like(dq_acc)
    for h in range(H):
        at = slice(h // GH * GF, h // GH * GF + GF)
        ebd[h * BLK : (h + 1) * BLK, :] = jnp.broadcast_to(e[h : h + 1, at], (BLK, GF))
    for s in range(CAP):
        listed, qb, kb = places[s]
        for copy in loads[s]:
            copy.wait()
        stat = jnp.where(qb == 0, whole[0:BLK], whole[BLK:])
        lse_s = jnp.where(listed, stat, -NEG)
        kf = keys_ref[s]
        qf = qf_ref[s]
        df = df_ref[s]
        for h in range(H):
            at = slice(h // GH * GF, h // GH * GF + GF)
            block = slice(h * BLK, (h + 1) * BLK)
            a = jnp.exp(logit_ref[s, h] - lse_s[:, h : h + 1])
            g = WL * a * (da_ref[s, h] - stat[:, 16 + h : 17 + h])
            gr = g.astype(BF16)
            gcat[:, block] = gr
            gstk[block, :] = gr
            astk[block, :] = a.astype(BF16)
            eh = e[h : h + 1, at]
            kbd[block, :] = kf[:, at] * eh
            qbd[block, :] = qf[:, at] * eh
            dbd[block, :] = df[:, at] * eh
        for g in range(G):
            at = slice(g * GF, (g + 1) * GF)
            block = slice(g * GJ, (g + 1) * GJ)
            dq_raw = dot(gcat[:, block], kbd[block, :])
            row_sum = dot(gcat[:, block], ebd[block, :])
            dq_acc[rows_of(qb), at] += fa[:, at] * dq_raw + fb[:, at] * row_sum * qf[:, at].astype(F32)
            dk_raw = dot(gstk[block, :], qbd[block, :], TN)
            col_sum = dot(gstk[block, :], ebd[block, :], TN)
            kg_acc[rows_of(kb), at] += fa[:, at] * dk_raw + fb[:, at] * col_sum * kf[:, at].astype(F32)
            kg_acc[rows_of(kb), FG + g * GF : FG + (g + 1) * GF] += dot(astk[block, :], dbd[block, :], TN)
    kg_ref[...] = kg_acc[...].astype(BF16)
    kg_copy = pltpu.make_async_copy(kg_ref, kg_hbm, sems.at[0])
    kg_copy.start()
    o_copy.wait()
    ahi, alo = split2(whole[:, 32:48])
    msg[:, 0:FG] = (o_ref[:, 0:FG].astype(F32) * (dot(ahi, e) + dot(alo, e))).astype(BF16)
    for h in range(H):
        at = slice(FG + h * PW, FG + (h + 1) * PW)
        msg[:, at] = (o_ref[:, at].astype(F32) * whole[:, 32 + h : 33 + h]).astype(BF16)
    msg[:, 2048:] = dq_acc[...].astype(BF16)
    core = lax.axis_index("col") % 2
    for x in range(4):
        keep_ref[x] = msg[pl.ds(pl.multiple_of((2 * x + core) * OWN, OWN), OWN), :]
        send_ref[x] = msg[pl.ds(pl.multiple_of((2 * x + 1 - core) * OWN, OWN), OWN), :]
    copies = fetch((send_ref, keep_ref, whole_ref), (send_hbm, keep_hbm, whole_hbm), sems, 1)
    for copy in [kg_copy] + copies:
        copy.wait()


def fold_kernel(keep_ref, got_ref, own_ref, one_ref, two_ref, three_ref):
    x = lax.axis_index("col") // 2
    for k, ref in enumerate((own_ref, one_ref, two_ref, three_ref)):
        at = (x + k) % 4
        ref[...] = (keep_ref[at].astype(F32) + got_ref[at].astype(F32)).astype(BF16)


def pair_out_kernel(codes_ref, whole_hbm, logit_hbm, da_hbm, dzp_hbm, out_ref, held, ga, sems, logit_ref, da_ref, dzp_ref, whole_ref, ins):
    (whole_copy,) = fetch((whole_hbm,), (whole_ref,), ins, 2 * CAP + 1)
    loads = []
    for s in range(CAP):
        loads.append(pltpu.make_async_copy(logit_hbm.at[s], logit_ref.at[s], ins.at[2 * s]))
        loads.append(pltpu.make_async_copy(da_hbm.at[s], da_ref.at[s], ins.at[2 * s + 1]))
    loads.insert(2, pltpu.make_async_copy(dzp_hbm, dzp_ref, ins.at[2 * CAP]))
    for copy in loads:
        copy.start()
    whole_copy.wait()
    for s in range(CAP):
        listed, qb, _ = slot_of(codes_ref, s)
        stat = whole_ref[rows_of(qb), :]
        lse_s = jnp.where(listed, stat, -NEG)
        for copy in loads[0:2] if s == 0 else loads[3:5]:
            copy.wait()
        for h in range(H):
            a = jnp.exp(logit_ref[s, h] - lse_s[:, h : h + 1])
            ga[h] = WL * a * (da_ref[s, h] - stat[:, 16 + h : 17 + h])
            ga[H + h] = a
        if s == 0:
            loads[2].wait()

        def some(k, carry, s=s, qb=qb):
            first = k * STEP
            zero = jnp.zeros((2 * H, PW), BF16)
            for i in range(0, STEP, 2):
                lhs = jnp.concatenate([ga[:, first + i, :], ga[:, first + i + 1, :]], axis=0).astype(BF16)
                one = dzp_ref[qb * BLK + first + i].astype(BF16)
                two = dzp_ref[qb * BLK + first + i + 1].astype(BF16)
                rhs = jnp.concatenate(
                    [jnp.concatenate([one, zero], axis=1), jnp.concatenate([zero, two], axis=1)], axis=0
                )
                found = dot(lhs, rhs, TN).astype(BF16)
                held[s * BLK + first + i] = found[:, :PW]
                held[s * BLK + first + i + 1] = found[:, PW:]

                if i % CHUNK == CHUNK - 2:
                    rows = pl.ds(pl.multiple_of(s * BLK + k * STEP + i + 2 - CHUNK, CHUNK), CHUNK)
                    at = s * (BLK // CHUNK) + k * (STEP // CHUNK) + i // CHUNK
                    pltpu.make_async_copy(held.at[rows], out_ref.at[rows], sems.at[at]).start()
            return carry

        lax.fori_loop(0, BLK // STEP, some, 0)
    for k in range(CHUNKS):
        pair_copy(held, out_ref, sems, k).wait()


def final_kernel(kg_ref, own_ref, one_ref, two_ref, three_ref, frame_q_ref, frame_k_ref, ow_hbm, up_ref, gq_ref, gk_ref, ow_ref, sems):
    (ow_copy,) = fetch((ow_hbm,), (ow_ref,), sems)
    total = kg_ref[0].astype(F32)
    for d in range(1, N_ROW):
        total = total + kg_ref[d].astype(F32)
    fk = frame_k_ref[...]
    fq = frame_q_ref[pl.ds(pl.multiple_of(lax.axis_index("col") * OWN, OWN), OWN), :]
    dk, dgk = ungrouped(total[:, :FG])
    dv, dgv = ungrouped(total[:, FG:])
    gk_ref[...] = jnp.concatenate(
        [dk, dv] + rotate_back(dgk, fk, False) + rotate_back(dgv, fk, False), axis=1
    ).astype(BF16)
    msg = (own_ref[...].astype(F32) + one_ref[...].astype(F32)) + (two_ref[...].astype(F32) + three_ref[...].astype(F32))
    scalar, parts = ungrouped(msg[:, :FG])
    head = jnp.concatenate([scalar] + rotate_back(parts, fq, True), axis=1).astype(BF16)
    tail = msg[:, FG:2048].astype(BF16)
    ow_copy.wait()
    up_ref[...] = (dot(head, ow_ref[0:F]) + dot(tail, ow_ref[F:])).astype(BF16)
    dq, dgq = ungrouped(msg[:, 2048:])
    gq_ref[...] = jnp.concatenate([dq] + rotate_back(dgq, fq, False), axis=1).astype(BF16)


SMEM = pl.BlockSpec(memory_space=pltpu.SMEM)
FULL = pl.BlockSpec(memory_space=pltpu.VMEM)
HBM = pl.BlockSpec(memory_space=pltpu.HBM)
DMA = pltpu.SemaphoreType.DMA


def call(kernel, name, ins, outs, scratch, mb, flops=0, nbytes=0):
    return pl.pallas_call(
        kernel,
        name=name,
        in_specs=ins,
        out_specs=[spec for _, spec in outs],
        out_shape=[shape for shape, _ in outs],
        scratch_shapes=scratch,
        compiler_params=pltpu.CompilerParams(vmem_limit_bytes=56 * MB if mb > 12 else mb * MB),
        cost_estimate=pl.CostEstimate(flops=flops, bytes_accessed=nbytes, transcendentals=0),
    )


def near(dims, kind):
    return jax.ShapeDtypeStruct(dims, kind), FULL


def far(dims, kind):
    return jax.ShapeDtypeStruct(dims, kind), HBM


def free(dims, kind):
    return jax.ShapeDtypeStruct(dims, kind), FULL


def on_device(queries, keys, frame_table, frame_index, pair_list, pair, pair_weight, point_weight, out_weight, cotangent):
    codes = pair_list.reshape(CAP)
    tiles = pair.reshape(CAP * BLK, BLK, PW)
    e = jnp.asarray(head_rows(), BF16)
    index = frame_index.reshape(1, NRES)
    sems = DMA((CHUNKS,))
    held = pltpu.VMEM((CAP * BLK, BLK, PW), BF16)
    table = pltpu.VMEM((12, NRES), F32)
    where = pltpu.VMEM((1, NRES), jnp.int32)
    planes = (CAP, H, BLK, BLK)

    key_wire, frame_k = call(
        key_kernel, "keys", [HBM] * 3, [far((N_ROW, OWN, 2 * FG), BF16), near((OWN, BLK), F32)],
        [pltpu.VMEM((BLK, BLK), F32), pltpu.VMEM((OWN, 2 * F), BF16), table, where, pltpu.VMEM((N_ROW, OWN, 2 * FG), BF16),
         DMA((3 + N_ROW,))], 56,
    )(keys, frame_table, index)
    key_all = lax.all_to_all(key_wire, "row", split_axis=0, concat_axis=0).reshape(KR, 2 * FG)

    half = pltpu.VMEM((CAP, BLK, FG), BF16)
    marks = pltpu.VMEM((48, FG), BF16)
    gammas = pltpu.VMEM((16, BLK), F32)
    rows = pltpu.VMEM((QR, FG), BF16)
    plane_buf = pltpu.VMEM(planes, F32)
    dzp_buf = pltpu.VMEM((QR, 2 * H, PW), F32)
    bz_buf = pltpu.VMEM((CAP, 2 * H, BLK, BLK), F32)
    qf, df, frame_q, gam, dzp, bz = call(
        prep_kernel, "prep", [SMEM] + [HBM] * 8,
        [far((QR, FG), BF16), far((QR, FG), BF16), far((QR, BLK), F32), far((16, BLK), F32),
         far((QR, 2 * H, PW), F32), far((CAP, 2 * H, BLK, BLK), F32)],
        [held, sems, table, where, pltpu.VMEM((1, H), F32), pltpu.VMEM((F, QR), BF16), pltpu.VMEM((QR, SW), BF16),
         pltpu.VMEM((2016, SW), BF16), pltpu.VMEM((H, PW), BF16), DMA((7,)),
         rows, rows, pltpu.VMEM((QR, BLK), F32), gammas, dzp_buf, bz_buf, DMA((CHUNKS + 5,))],
        56, flops=3_000_000_000, nbytes=30_000_000,
    )(codes, queries.T, pair_weight.T, point_weight.reshape(1, H), frame_table, index, cotangent, out_weight, tiles)

    mine, logit, da, stat = call(
        logit_kernel, "logit", [SMEM] + [HBM] * 6, [far((32, QR), F32), far(planes, F32), far(planes, F32), far((N_COL, 32, QR), F32)],
        [pltpu.VMEM((CAP, BLK, 2 * FG), BF16), half, half, marks, gammas, pltpu.VMEM((32, QR), F32), bz_buf, plane_buf,
         plane_buf, DMA((10,)), DMA((H,))], 56,
    )(codes, key_all, qf, df, e, gam, bz)

    stat_all = lax.all_to_all(stat, "col", split_axis=0, concat_axis=0)

    (out,) = call(
        out_kernel, "local_out", [SMEM] + [HBM] * 5, [far((QR, 2048), BF16)],
        [held, pltpu.VMEM((H, BLK, BLK), F32), pltpu.VMEM((H, BLK, PW), F32), pltpu.VMEM((BLK, HJ), BF16),
         pltpu.VMEM((HJ, GF), BF16), sems, plane_buf, half, pltpu.VMEM((32, QR), F32), marks,
         pltpu.VMEM((QR, 2048), F32), pltpu.VMEM((QR, 2048), BF16), DMA((6,))], 56, flops=2_000_000_000, nbytes=20_000_000,
    )(codes, tiles, logit, key_all, mine, e)

    whole, keep, kg, send = call(
        back_kernel, "back", [SMEM] + [HBM] * 10,
        [far((QR, BLK), F32), far((4, OWN, 2560), BF16), far((KR, 2 * FG), BF16), far((4, OWN, 2560), BF16)],
        [pltpu.VMEM((32, QR), F32), pltpu.VMEM((N_COL, 32, QR), F32), half, half, half, marks, gammas, plane_buf, plane_buf,
         pltpu.VMEM((QR, 2048), BF16), DMA((21,)),
         pltpu.VMEM((QR, BLK), F32), pltpu.VMEM((4, OWN, 2560), BF16), pltpu.VMEM((KR, 2 * FG), BF16),
         pltpu.VMEM((4, OWN, 2560), BF16), DMA((4,)),
         pltpu.VMEM((KR, 2 * FG), F32), pltpu.VMEM((BLK, HJ), BF16), pltpu.VMEM((HJ, BLK), BF16),
         pltpu.VMEM((HJ, BLK), BF16), pltpu.VMEM((HJ, GF), BF16), pltpu.VMEM((HJ, GF), BF16),
         pltpu.VMEM((HJ, GF), BF16), pltpu.VMEM((HJ, GF), BF16), pltpu.VMEM((QR, FG), F32),
         pltpu.VMEM((QR, 2560), BF16)], 56,
    )(codes, mine, stat_all, key_all, qf, df, e, gam, logit, da, out)

    kg_all = lax.all_to_all(kg.reshape(N_ROW, OWN, 2 * FG), "row", split_axis=0, concat_axis=0)
    got = lax.ppermute(send, "col", [(d, d ^ 1) for d in range(N_COL)])
    own, *away = call(
        fold_kernel, "fold", [FULL] * 2, [near((OWN, 2560), BF16)] + [free((OWN, 2560), BF16)] * 3, [], 4
    )(keep, got)
    came = [
        lax.ppermute(part, "col", [(d, (d + 2 * k) % N_COL) for d in range(N_COL)])
        for k, part in enumerate(away, 1)
    ]

    (grad_tiles,) = call(
        pair_out_kernel, "pair_out", [SMEM] + [HBM] * 4, [far((CAP * BLK, BLK, PW), BF16)],
        [held, pltpu.VMEM((2 * H, BLK, BLK), F32), sems, plane_buf, plane_buf, dzp_buf,
         pltpu.VMEM((QR, BLK), F32), DMA((2 * CAP + 2,))], 56, flops=4_000_000_000, nbytes=30_000_000,
    )(codes, whole, logit, da, dzp)

    update, grad_queries, grad_keys = call(
        final_kernel, "final", [FULL] * 7 + [HBM],
        [free((OWN, SW), BF16), free((OWN, F), BF16), free((OWN, 2 * F), BF16)],
        [pltpu.VMEM((2016, SW), BF16), DMA((1,))], 12,
    )(kg_all, own, *came, frame_q, frame_k, out_weight)
    return update, grad_queries, grad_keys, grad_tiles.reshape(pair.shape)


def solution(mesh):
    in_specs = (
        P("row", None),
        P(("col", "row"), None),
        P(),
        P(),
        P("row", "col", None),
        P("row", "col", None, None, None, None),
        P(),
        P(),
        P(),
        P("row", None),
    )
    out_specs = (
        P(("row", "col"), None),
        P(("row", "col"), None),
        P(("col", "row"), None),
        P("row", "col", None, None, None, None),
    )
    return jax.shard_map(on_device, mesh=mesh, in_specs=in_specs, out_specs=out_specs, check_vma=False)
```

```python
import functools
import math

import jax
import jax.numpy as jnp
import numpy as np
from jax import lax
from jax.experimental import pallas as pl
from jax.experimental.pallas import tpu as pltpu
from jax.sharding import PartitionSpec as P

H = 12
C = 16
PV = 8
PW = 128
BLK = 128
SW = 384
QR = 256
KR = 512
NRES = 4096
KEYB = 4
CAP = 2
F = 480
WS = 192
WP = 288
HJ = H * BLK
GJ = 6 * BLK
N_ROW = 16
N_COL = 8
OWN = 32
EMPTY = 8
NEG = -1e30
SC = 1.0 / math.sqrt(C)
WC = math.sqrt(2.0 / 72.0)
WL = math.sqrt(1.0 / 3.0)
F32 = jnp.float32
BF16 = jnp.bfloat16
MB = 1024 * 1024
G = 2
GH = 6
GF = 256
FG = G * GF
CHUNK = 32
STEP = 128

NN = (((1,), (0,)), ((), ()))
NT = (((1,), (1,)), ((), ()))
TN = (((0,), (0,)), ((), ()))


def head_rows():
    f = np.arange(FG)
    group, at = f // GF, f % GF
    head = np.where(at < 96, at // C, ((at - 96) % 48) // PV) + GH * group
    mine = (head[None, :] == np.arange(16)[:, None]) & (at < 240)[None, :]
    scalar, point = mine & (at < 96)[None, :], mine & (at >= 96)[None, :]
    return np.concatenate([scalar, point, mine], axis=0).astype(np.float32)


def dot(a, b, dims=NN):
    return lax.dot_general(a, b, dims, preferred_element_type=F32)


def split3(x):
    hi = x.astype(BF16)
    rest = x - hi.astype(F32)
    mid = rest.astype(BF16)
    lo = (rest - mid.astype(F32)).astype(BF16)
    return hi, mid, lo


def split2(x):
    hi = x.astype(BF16)
    return hi, (x - hi.astype(F32)).astype(BF16)


def rotate(parts, frame, shift):
    out = []
    for a in range(3):
        y = sum(frame[:, 3 * a + b : 3 * a + b + 1] * parts[b] for b in range(3))
        if shift:
            y = y + frame[:, 9 + a : 10 + a]
        out.append(y)
    return out


def rotate_back(parts, frame, shift):
    if shift:
        parts = [parts[a] - frame[:, 9 + a : 10 + a] for a in range(3)]
    return [sum(frame[:, 3 * a + b : 3 * a + b + 1] * parts[a] for a in range(3)) for b in range(3)]


def components(x):
    return [x[:, 96 * b : 96 * b + 96] for b in range(3)]


def grouped(scalar, parts):
    pad = jnp.zeros((scalar.shape[0], 16), F32)
    pieces = []
    for g in range(G):
        pieces.append(scalar[:, 96 * g : 96 * g + 96])
        pieces.extend(part[:, 48 * g : 48 * g + 48] for part in parts)
        pieces.append(pad)
    return jnp.concatenate(pieces, axis=1).astype(BF16)


def ungrouped(x):
    scalar = jnp.concatenate([x[:, GF * g : GF * g + 96] for g in range(G)], axis=1)
    parts = []
    for a in range(3):
        first = 96 + 48 * a
        parts.append(jnp.concatenate([x[:, GF * g + first : GF * g + first + 48] for g in range(G)], axis=1))
    return scalar, parts


def slot_of(codes_ref, s):
    code = codes_ref[s]
    listed = code < EMPTY
    safe = jnp.where(listed, code, 0)
    return listed, safe // KEYB, safe % KEYB


def rows_of(block):
    return pl.ds(pl.multiple_of(block * BLK, BLK), BLK)


def fetch(refs, held, sems, first=0):
    copies = [pltpu.make_async_copy(ref, buf, sems.at[first + n]) for n, (ref, buf) in enumerate(zip(refs, held))]
    for copy in copies:
        copy.start()
    return copies


def look_up(table_ref, ids):
    count = ids.shape[1]
    found = jnp.zeros((48, count), F32)
    step = 512
    pad = jnp.zeros((4, step), F32)
    for first in range(0, NRES, step):
        table = jnp.concatenate([table_ref[:, first : first + step], pad], axis=0)
        table = jnp.concatenate(split3(table), axis=0)
        at = lax.broadcasted_iota(jnp.int32, (step, count), 0) + first
        found = found + dot(table, jnp.where(at == ids, 1.0, 0.0).astype(BF16))
    return found[0:16] + found[16:32] + found[32:48]


def key_kernel(keys_hbm, table_hbm, index_hbm, wire_hbm, frame_ref, held_ref, keys_ref, table_ref, index_ref, wire_ref, sems):
    copies = fetch((keys_hbm, table_hbm, index_hbm), (keys_ref, table_ref, index_ref), sems)
    for copy in copies:
        copy.wait()
    at = lax.axis_index("col") * N_ROW + lax.axis_index("row")
    window = at // 4
    ids = index_ref[:, pl.ds(pl.multiple_of(window * BLK, BLK), BLK)]
    held_ref[...] = jnp.transpose(jnp.concatenate([look_up(table_ref, ids), jnp.zeros((112, BLK), F32)], axis=0))
    frame = held_ref[pl.ds(pl.multiple_of((at % 4) * OWN, OWN), OWN), :]
    frame_ref[...] = frame
    keys = keys_ref[...].astype(F32)
    gk = rotate(components(keys[:, 2 * WS : 2 * WS + WP]), frame, True)
    gv = rotate(components(keys[:, 2 * WS + WP :]), frame, True)
    wire = jnp.concatenate([grouped(keys[:, :WS], gk), grouped(keys[:, WS : 2 * WS], gv)], axis=1)
    for d in range(N_ROW):
        wire_ref[d] = wire
    copies = [pltpu.make_async_copy(wire_ref.at[pl.ds(4 * d, 4)], wire_hbm.at[pl.ds(4 * d, 4)], sems.at[3 + d]) for d in range(4)]
    for copy in copies:
        copy.start()
    for copy in copies:
        copy.wait()


def pair_copy(pair_ref, held, sems, k):
    rows = pl.ds(k * CHUNK, CHUNK)
    return pltpu.make_async_copy(pair_ref.at[rows], held.at[rows], sems.at[k])


CHUNKS = CAP * BLK // CHUNK


def prep_kernel(codes_ref, q_hbm, pw_hbm, gam_hbm, table_hbm, index_hbm, cot_hbm, ow_hbm, pair_ref,
                qf_hbm, df_hbm, frame_hbm, gamma_hbm, dzp_hbm, bz_hbm,
                held, sems, table_ref, index_ref, gam_ref, q_ref, cot_ref, ow_ref, pw_ref, more,
                qf_ref, df_ref, frame_ref, gamma_ref, dzp_ref, bz_ref, outs):
    loads = fetch((table_hbm, index_hbm, gam_hbm, q_hbm, cot_hbm, ow_hbm, pw_hbm),
                  (table_ref, index_ref, gam_ref, q_ref, cot_ref, ow_ref, pw_ref), more)
    for k in range(CHUNKS):
        pair_copy(pair_ref, held, sems, k).start()
    row = lax.axis_index("row")
    for copy in loads[:3]:
        copy.wait()
    frame_t = look_up(table_ref, index_ref[:, pl.ds(pl.multiple_of(row * QR, QR), QR)])
    frame = jnp.transpose(jnp.concatenate([frame_t, jnp.zeros((112, QR), F32)], axis=0))
    frame_ref[...] = frame
    raw = gam_ref[...]
    soft = jnp.maximum(raw, 0.0) + jnp.log(1.0 + jnp.exp(-jnp.abs(raw)))
    diag = lax.broadcasted_iota(jnp.int32, (16, H), 0) == lax.broadcasted_iota(jnp.int32, (16, H), 1)
    gamma_ref[...] = jnp.broadcast_to(jnp.sum(jnp.where(diag, soft, 0.0), axis=1, keepdims=True), (16, BLK))
    for copy in loads[3:]:
        copy.wait()
    q = jnp.transpose(q_ref[...].astype(F32))
    qf_ref[...] = grouped(q[:, :WS], rotate(components(q[:, WS:]), frame, True))
    cot = cot_ref[...]
    head = dot(cot, ow_ref[0:F], NT).astype(BF16).astype(F32)
    df_ref[...] = grouped(head[:, :WS], rotate(components(head[:, WS:]), frame, False))
    tail = dot(cot, ow_ref[F:], NT).astype(BF16).astype(F32)
    pwt = pw_ref[...].astype(F32)
    for h in range(H):
        dzp_ref[:, h, :] = jnp.broadcast_to(pwt[h : h + 1], (QR, PW))
        dzp_ref[:, H + h, :] = tail[:, h * PW : (h + 1) * PW]
    stores = fetch((qf_ref, df_ref, frame_ref, gamma_ref, dzp_ref), (qf_hbm, df_hbm, frame_hbm, gamma_hbm, dzp_hbm), outs, CHUNKS)

    def bz_copy(s, k):
        rows = pl.ds(k * CHUNK, CHUNK)
        return pltpu.make_async_copy(bz_ref.at[s, :, rows], bz_hbm.at[s, :, rows], outs.at[s * (BLK // CHUNK) + k])

    for s in range(CAP):
        _, qb, _ = slot_of(codes_ref, s)

        def some(k, carry, s=s, qb=qb):
            for c in range(STEP // CHUNK):
                rows = pl.ds(pl.multiple_of(s * BLK + k * STEP + c * CHUNK, CHUNK), CHUNK)
                at = s * (BLK // CHUNK) + k * (STEP // CHUNK) + c
                pltpu.make_async_copy(pair_ref.at[rows], held.at[rows], sems.at[at]).wait()
            first = k * STEP
            for i in range(0, STEP, 2):
                lhs = dzp_ref[pl.ds(qb * BLK + first + i, 2)].reshape(4 * H, PW).astype(BF16)
                z = held[pl.ds(s * BLK + first + i, 2)].reshape(2 * BLK, PW)
                found = dot(lhs, z, NT)
                bz_ref[s, :, first + i, :] = found[0 : 2 * H, 0:BLK]
                bz_ref[s, :, first + i + 1, :] = found[2 * H :, BLK:]

            for c in range(STEP // CHUNK):
                bz_copy(s, k * (STEP // CHUNK) + c).start()
            return carry

        lax.fori_loop(0, BLK // STEP, some, 0)
    for copy in stores:
        copy.wait()
    for s in range(CAP):
        for k in range(BLK // CHUNK):
            bz_copy(s, k).wait()


def logit_kernel(codes_ref, keys_hbm, qf_hbm, df_hbm, e_hbm, gam_hbm, bz_hbm, mine_hbm, logit_hbm, da_hbm, stat_hbm,
                 keys_ref, qf_ref, df_ref, e_ref, gam_ref, mine_ref, bz_ref, logit_ref, da_ref, ins, outs):
    places = [slot_of(codes_ref, s) for s in range(CAP)]
    small = fetch((e_hbm, gam_hbm), (e_ref, gam_ref), ins)
    loads = []
    for s, (_, qb, kb) in enumerate(places):
        loads.append(fetch(
            (keys_hbm.at[rows_of(kb)], qf_hbm.at[rows_of(qb)], df_hbm.at[rows_of(qb)], bz_hbm.at[s]),
            (keys_ref.at[s], qf_ref.at[s], df_ref.at[s], bz_ref.at[s]), ins, 2 + 4 * s,
        ))
    stores = []
    for copy in small:
        copy.wait()
    e = e_ref[...]
    lane = lax.broadcasted_iota(jnp.int32, (BLK, BLK), 1)
    stats = []
    for s in range(CAP):
        listed, qb, kb = places[s]
        for copy in loads[s][:3]:
            copy.wait()
        kf = keys_ref[s, :, 0:FG]
        vf = keys_ref[s, :, FG:]
        qf = qf_ref[s]
        df = df_ref[s]
        qhi, qlo = split2(jnp.square(qf.astype(F32)))
        khi, klo = split2(jnp.square(kf.astype(F32)))
        ep = e[16:32]
        qn = dot(qhi, ep, NT) + dot(qlo, ep, NT)
        kn = dot(ep, khi, NT) + dot(ep, klo, NT)
        held = jnp.zeros((BLK, BLK), F32)
        loads[s][3].wait()
        for h in range(0, H, 2):
            at = slice(h // GH * GF, h // GH * GF + GF)
            kg = kf[:, at]
            vg = vf[:, at]
            qg = qf[:, at]
            das = dot(df[:, at], jnp.concatenate([vg * e[32 + h : 33 + h, at], vg * e[33 + h : 34 + h, at]], axis=0), NT)
            for n in range(2):
                u = h + n
                both = dot(qg, jnp.concatenate([kg * e[u : u + 1, at], kg * e[16 + u : 17 + u, at]], axis=0), NT)
                dist = qn[:, u : u + 1] + kn[u : u + 1, :] - 2.0 * both[:, BLK:]
                logit = (WL * SC) * both[:, :BLK] + WL * bz_ref[s, u] - (0.5 * WL * WC) * gam_ref[u : u + 1] * dist
                da = bz_ref[s, H + u] + das[:, n * BLK : (n + 1) * BLK]
                logit_ref[s, u] = logit
                da_ref[s, u] = da
                top = jnp.max(logit, axis=1, keepdims=True)
                p = jnp.exp(logit - top)
                total = jnp.sum(p, axis=1, keepdims=True)
                mean = jnp.sum(p * da, axis=1, keepdims=True) / total
                held = jnp.where(lane == u, top + jnp.log(total), held)
                held = jnp.where(lane == 16 + u, mean, held)
            if h % 4 == 2:
                some = pl.ds(h - 2, 4)
                for n, (ref, hbm) in enumerate(((logit_ref, logit_hbm), (da_ref, da_hbm))):
                    at = (2 * s + n) * (H // 4) + h // 4
                    stores.append(pltpu.make_async_copy(ref.at[s, some], hbm.at[s, some], outs.at[at]))
                    stores[-1].start()
        stats.append((listed, qb, jnp.transpose(held)))
    for b in range(2):
        lse = []
        for listed, qb, held in stats:
            lse.append(jnp.where(jnp.logical_and(listed, qb == b), held[0:16], NEG))
        top = jnp.maximum(lse[0], lse[1])
        w0 = jnp.exp(lse[0] - top)
        w1 = jnp.exp(lse[1] - top)
        total = w0 + w1
        merged = jnp.concatenate(
            [top + jnp.log(total), (w0 * stats[0][2][16:32] + w1 * stats[1][2][16:32]) / total], axis=0
        )
        mine_ref[:, b * BLK : (b + 1) * BLK] = merged
    stores.extend(fetch([mine_ref] * (N_COL + 1), [mine_hbm] + [stat_hbm.at[d] for d in range(N_COL)], ins))
    for copy in stores:
        copy.wait()


def out_kernel(codes_ref, pair_ref, logit_hbm, keys_hbm, stat_hbm, e_hbm, o_hbm, held, p_ref, nz_ref, cat_ref, bd_ref, sems,
               logit_ref, keys_ref, stat_ref, e_ref, o_ref, low_ref, ins):
    places = [slot_of(codes_ref, s) for s in range(CAP)]
    loads = fetch((stat_hbm, e_hbm), (stat_ref, e_ref), ins)
    for s, (_, _, kb) in enumerate(places):
        loads.extend(fetch((logit_hbm.at[s], keys_hbm.at[rows_of(kb), pl.ds(FG, FG)]), (logit_ref.at[s], keys_ref.at[s]), ins, 2 + 2 * s))
    for k in range(CHUNKS):
        pair_copy(pair_ref, held, sems, k).start()
    loads[0].wait()
    loads[1].wait()
    o_ref[...] = jnp.zeros_like(o_ref)
    for s in range(CAP):
        listed, qb, kb = places[s]
        lse = jnp.transpose(jnp.concatenate([stat_ref[:, rows_of(qb)], jnp.zeros((96, BLK), F32)], axis=0))
        lse = jnp.where(listed, lse, -NEG)
        loads[2 + 2 * s].wait()
        loads[3 + 2 * s].wait()
        vf = keys_ref[s]
        for h in range(H):
            at = slice(h // GH * GF, h // GH * GF + GF)
            p = jnp.exp(logit_ref[s, h] - lse[:, h : h + 1])
            p_ref[h] = p
            cat_ref[:, h * BLK : (h + 1) * BLK] = p.astype(BF16)
            bd_ref[h * BLK : (h + 1) * BLK, :] = vf[:, at] * e_ref[32 + h : 33 + h, at]
        for g in range(G):
            at = slice(g * GJ, (g + 1) * GJ)
            o_ref[rows_of(qb), g * GF : (g + 1) * GF] += dot(cat_ref[:, at], bd_ref[at, :])

        def some(k, carry, s=s):
            for c in range(STEP // CHUNK):
                rows = pl.ds(pl.multiple_of(s * BLK + k * STEP + c * CHUNK, CHUNK), CHUNK)
                at = s * (BLK // CHUNK) + k * (STEP // CHUNK) + c
                pltpu.make_async_copy(pair_ref.at[rows], held.at[rows], sems.at[at]).wait()
            first = k * STEP
            zero = jnp.zeros((H, BLK), F32)
            for i in range(0, STEP, 2):
                w = jnp.concatenate(
                    [
                        jnp.concatenate([p_ref[:, first + i, :], zero], axis=1),
                        jnp.concatenate([zero, p_ref[:, first + i + 1, :]], axis=1),
                    ],
                    axis=0,
                ).astype(BF16)
                found = dot(w, held[pl.ds(s * BLK + first + i, 2)].reshape(2 * BLK, PW))
                nz_ref[:, first + i, :] = found[0:H]
                nz_ref[:, first + i + 1, :] = found[H:]
            return carry

        lax.fori_loop(0, BLK // STEP, some, 0)
        for h in range(H):
            o_ref[rows_of(qb), FG + h * PW : FG + (h + 1) * PW] += nz_ref[h]
    low_ref[...] = o_ref[...].astype(BF16)
    (copy,) = fetch((low_ref,), (o_hbm,), ins)
    copy.wait()


def back_kernel(codes_ref, stat_hbm, stats_hbm, keys_hbm, qf_hbm, df_hbm, e_hbm, gam_hbm, logit_hbm, da_hbm, o_hbm,
                whole_hbm, keep_hbm, kg_hbm, send_hbm,
                mine_ref, all_ref, keys_ref, qf_ref, df_ref, e_ref, gam_ref, logit_ref, da_ref, o_ref, ins,
                whole_ref, keep_ref, kg_ref, send_ref, sems, kg_acc, gcat, gstk, astk, kbd, qbd, dbd, ebd, dq_acc, msg):
    places = [slot_of(codes_ref, s) for s in range(CAP)]
    small = fetch((stat_hbm, stats_hbm, e_hbm, gam_hbm), (mine_ref, all_ref, e_ref, gam_ref), ins)
    loads = []
    for s, (_, qb, kb) in enumerate(places):
        loads.append(fetch(
            (logit_hbm.at[s], da_hbm.at[s], keys_hbm.at[rows_of(kb), pl.ds(0, FG)], qf_hbm.at[rows_of(qb)], df_hbm.at[rows_of(qb)]),
            (logit_ref.at[s], da_ref.at[s], keys_ref.at[s], qf_ref.at[s], df_ref.at[s]), ins, 10 + 5 * s,
        ))
    (o_copy,) = fetch((o_hbm,), (o_ref,), ins, 20)
    for copy in small:
        copy.wait()
    held = [all_ref[d] for d in range(N_COL)]
    top = held[0][0:16]
    for d in range(1, N_COL):
        top = jnp.maximum(top, held[d][0:16])
    total = jnp.zeros((16, QR), F32)
    mean = jnp.zeros((16, QR), F32)
    for d in range(N_COL):
        w = jnp.exp(held[d][0:16] - top)
        total = total + w
        mean = mean + w * held[d][16:32]
    lse = top + jnp.log(total)
    delta = mean / total
    alpha = jnp.exp(mine_ref[0:16] - lse)
    whole_t = jnp.concatenate([lse, delta, alpha, jnp.zeros((80, QR), F32)], axis=0)
    whole = jnp.transpose(whole_t)
    whole_ref[...] = whole
    e = e_ref[32:48]
    gam_f = jnp.sum(e.astype(F32) * gam_ref[:, 0:1], axis=0, keepdims=True)
    point = jnp.sum(e_ref[16:32].astype(F32), axis=0, keepdims=True)
    scalar = jnp.sum(e_ref[0:16].astype(F32), axis=0, keepdims=True)
    fa = WC * gam_f * point + SC * scalar
    fb = -WC * gam_f * point
    kg_acc[...] = jnp.zeros_like(kg_acc)
    dq_acc[...] = jnp.zeros_like(dq_acc)
    for h in range(H):
        at = slice(h // GH * GF, h // GH * GF + GF)
        ebd[h * BLK : (h + 1) * BLK, :] = jnp.broadcast_to(e[h : h + 1, at], (BLK, GF))
    for s in range(CAP):
        listed, qb, kb = places[s]
        for copy in loads[s]:
            copy.wait()
        stat = jnp.where(qb == 0, whole[0:BLK], whole[BLK:])
        lse_s = jnp.where(listed, stat, -NEG)
        kf = keys_ref[s]
        qf = qf_ref[s]
        df = df_ref[s]
        for h in range(H):
            at = slice(h // GH * GF, h // GH * GF + GF)
            block = slice(h * BLK, (h + 1) * BLK)
            a = jnp.exp(logit_ref[s, h] - lse_s[:, h : h + 1])
            g = WL * a * (da_ref[s, h] - stat[:, 16 + h : 17 + h])
            gr = g.astype(BF16)
            gcat[:, block] = gr
            gstk[block, :] = gr
            astk[block, :] = a.astype(BF16)
            eh = e[h : h + 1, at]
            kbd[block, :] = kf[:, at] * eh
            qbd[block, :] = qf[:, at] * eh
            dbd[block, :] = df[:, at] * eh
        for g in range(G):
            at = slice(g * GF, (g + 1) * GF)
            block = slice(g * GJ, (g + 1) * GJ)
            dq_raw = dot(gcat[:, block], kbd[block, :])
            row_sum = dot(gcat[:, block], ebd[block, :])
            dq_acc[rows_of(qb), at] += fa[:, at] * dq_raw + fb[:, at] * row_sum * qf[:, at].astype(F32)
            dk_raw = dot(gstk[block, :], qbd[block, :], TN)
            col_sum = dot(gstk[block, :], ebd[block, :], TN)
            kg_acc[rows_of(kb), at] += fa[:, at] * dk_raw + fb[:, at] * col_sum * kf[:, at].astype(F32)
            kg_acc[rows_of(kb), FG + g * GF : FG + (g + 1) * GF] += dot(astk[block, :], dbd[block, :], TN)
    kg_ref[...] = kg_acc[...].astype(BF16)
    kg_copy = pltpu.make_async_copy(kg_ref, kg_hbm, sems.at[0])
    kg_copy.start()
    o_copy.wait()
    ahi, alo = split2(whole[:, 32:48])
    msg[:, 0:FG] = (o_ref[:, 0:FG].astype(F32) * (dot(ahi, e) + dot(alo, e))).astype(BF16)
    for h in range(H):
        at = slice(FG + h * PW, FG + (h + 1) * PW)
        msg[:, at] = (o_ref[:, at].astype(F32) * whole[:, 32 + h : 33 + h]).astype(BF16)
    msg[:, 2048:] = dq_acc[...].astype(BF16)
    core = lax.axis_index("col") % 2
    for x in range(4):
        keep_ref[x] = msg[pl.ds(pl.multiple_of((2 * x + core) * OWN, OWN), OWN), :]
        send_ref[x] = msg[pl.ds(pl.multiple_of((2 * x + 1 - core) * OWN, OWN), OWN), :]
    copies = fetch((send_ref, keep_ref, whole_ref), (send_hbm, keep_hbm, whole_hbm), sems, 1)
    for copy in [kg_copy] + copies:
        copy.wait()


def fold_kernel(keep_ref, got_ref, own_ref, one_ref, two_ref, three_ref):
    x = lax.axis_index("col") // 2
    for k, ref in enumerate((own_ref, one_ref, two_ref, three_ref)):
        at = (x + k) % 4
        ref[...] = (keep_ref[at].astype(F32) + got_ref[at].astype(F32)).astype(BF16)


def pair_out_kernel(codes_ref, whole_hbm, logit_hbm, da_hbm, dzp_hbm, out_ref, held, ga, sems, logit_ref, da_ref, dzp_ref, whole_ref, ins):
    (whole_copy,) = fetch((whole_hbm,), (whole_ref,), ins, 2 * CAP + 1)
    loads = []
    for s in range(CAP):
        loads.append(pltpu.make_async_copy(logit_hbm.at[s], logit_ref.at[s], ins.at[2 * s]))
        loads.append(pltpu.make_async_copy(da_hbm.at[s], da_ref.at[s], ins.at[2 * s + 1]))
    loads.insert(2, pltpu.make_async_copy(dzp_hbm, dzp_ref, ins.at[2 * CAP]))
    for copy in loads:
        copy.start()
    whole_copy.wait()
    for s in range(CAP):
        listed, qb, _ = slot_of(codes_ref, s)
        stat = whole_ref[rows_of(qb), :]
        lse_s = jnp.where(listed, stat, -NEG)
        for copy in loads[0:2] if s == 0 else loads[3:5]:
            copy.wait()
        for h in range(H):
            a = jnp.exp(logit_ref[s, h] - lse_s[:, h : h + 1])
            ga[h] = WL * a * (da_ref[s, h] - stat[:, 16 + h : 17 + h])
            ga[H + h] = a
        if s == 0:
            loads[2].wait()

        def some(k, carry, s=s, qb=qb):
            first = k * STEP
            zero = jnp.zeros((2 * H, PW), BF16)
            for i in range(0, STEP, 2):
                lhs = jnp.concatenate([ga[:, first + i, :], ga[:, first + i + 1, :]], axis=0).astype(BF16)
                one = dzp_ref[qb * BLK + first + i].astype(BF16)
                two = dzp_ref[qb * BLK + first + i + 1].astype(BF16)
                rhs = jnp.concatenate(
                    [jnp.concatenate([one, zero], axis=1), jnp.concatenate([zero, two], axis=1)], axis=0
                )
                found = dot(lhs, rhs, TN).astype(BF16)
                held[s * BLK + first + i] = found[:, :PW]
                held[s * BLK + first + i + 1] = found[:, PW:]

                if i % CHUNK == CHUNK - 2:
                    rows = pl.ds(pl.multiple_of(s * BLK + k * STEP + i + 2 - CHUNK, CHUNK), CHUNK)
                    at = s * (BLK // CHUNK) + k * (STEP // CHUNK) + i // CHUNK
                    pltpu.make_async_copy(held.at[rows], out_ref.at[rows], sems.at[at]).start()
            return carry

        lax.fori_loop(0, BLK // STEP, some, 0)
    for k in range(CHUNKS):
        pair_copy(held, out_ref, sems, k).wait()


def final_kernel(kg_ref, own_ref, one_ref, two_ref, three_ref, frame_q_ref, frame_k_ref, ow_hbm, up_ref, gq_ref, gk_ref, ow_ref, sems):
    (ow_copy,) = fetch((ow_hbm,), (ow_ref,), sems)
    total = kg_ref[0].astype(F32)
    for d in range(1, N_ROW):
        total = total + kg_ref[d].astype(F32)
    fk = frame_k_ref[...]
    fq = frame_q_ref[pl.ds(pl.multiple_of(lax.axis_index("col") * OWN, OWN), OWN), :]
    dk, dgk = ungrouped(total[:, :FG])
    dv, dgv = ungrouped(total[:, FG:])
    gk_ref[...] = jnp.concatenate(
        [dk, dv] + rotate_back(dgk, fk, False) + rotate_back(dgv, fk, False), axis=1
    ).astype(BF16)
    msg = (own_ref[...].astype(F32) + one_ref[...].astype(F32)) + (two_ref[...].astype(F32) + three_ref[...].astype(F32))
    scalar, parts = ungrouped(msg[:, :FG])
    head = jnp.concatenate([scalar] + rotate_back(parts, fq, True), axis=1).astype(BF16)
    tail = msg[:, FG:2048].astype(BF16)
    ow_copy.wait()
    up_ref[...] = (dot(head, ow_ref[0:F]) + dot(tail, ow_ref[F:])).astype(BF16)
    dq, dgq = ungrouped(msg[:, 2048:])
    gq_ref[...] = jnp.concatenate([dq] + rotate_back(dgq, fq, False), axis=1).astype(BF16)


SMEM = pl.BlockSpec(memory_space=pltpu.SMEM)
FULL = pl.BlockSpec(memory_space=pltpu.VMEM)
HBM = pl.BlockSpec(memory_space=pltpu.HBM)
DMA = pltpu.SemaphoreType.DMA


def call(kernel, name, ins, outs, scratch, mb, flops=0, nbytes=0):
    return pl.pallas_call(
        kernel,
        name=name,
        in_specs=ins,
        out_specs=[spec for _, spec in outs],
        out_shape=[shape for shape, _ in outs],
        scratch_shapes=scratch,
        compiler_params=pltpu.CompilerParams(vmem_limit_bytes=56 * MB if mb > 12 else mb * MB),
        cost_estimate=pl.CostEstimate(flops=flops, bytes_accessed=nbytes, transcendentals=0),
    )


def near(dims, kind):
    return jax.ShapeDtypeStruct(dims, kind), FULL


def far(dims, kind):
    return jax.ShapeDtypeStruct(dims, kind), HBM


def free(dims, kind):
    return jax.ShapeDtypeStruct(dims, kind), FULL


def on_device(queries, keys, frame_table, frame_index, pair_list, pair, pair_weight, point_weight, out_weight, cotangent):
    codes = pair_list.reshape(CAP)
    tiles = pair.reshape(CAP * BLK, BLK, PW)
    e = jnp.asarray(head_rows(), BF16)
    index = frame_index.reshape(1, NRES)
    sems = DMA((CHUNKS,))
    held = pltpu.VMEM((CAP * BLK, BLK, PW), BF16)
    table = pltpu.VMEM((12, NRES), F32)
    where = pltpu.VMEM((1, NRES), jnp.int32)
    planes = (CAP, H, BLK, BLK)

    key_wire, frame_k = call(
        key_kernel, "keys", [HBM] * 3, [far((N_ROW, OWN, 2 * FG), BF16), near((OWN, BLK), F32)],
        [pltpu.VMEM((BLK, BLK), F32), pltpu.VMEM((OWN, 2 * F), BF16), table, where, pltpu.VMEM((N_ROW, OWN, 2 * FG), BF16),
         DMA((3 + N_ROW,))], 56,
    )(keys, frame_table, index)
    key_all = lax.all_to_all(key_wire, "row", split_axis=0, concat_axis=0).reshape(KR, 2 * FG)

    half = pltpu.VMEM((CAP, BLK, FG), BF16)
    marks = pltpu.VMEM((48, FG), BF16)
    gammas = pltpu.VMEM((16, BLK), F32)
    rows = pltpu.VMEM((QR, FG), BF16)
    plane_buf = pltpu.VMEM(planes, F32)
    dzp_buf = pltpu.VMEM((QR, 2 * H, PW), F32)
    bz_buf = pltpu.VMEM((CAP, 2 * H, BLK, BLK), F32)
    qf, df, frame_q, gam, dzp, bz = call(
        prep_kernel, "prep", [SMEM] + [HBM] * 8,
        [far((QR, FG), BF16), far((QR, FG), BF16), far((QR, BLK), F32), far((16, BLK), F32),
         far((QR, 2 * H, PW), F32), far((CAP, 2 * H, BLK, BLK), F32)],
        [held, sems, table, where, pltpu.VMEM((1, H), F32), pltpu.VMEM((F, QR), BF16), pltpu.VMEM((QR, SW), BF16),
         pltpu.VMEM((2016, SW), BF16), pltpu.VMEM((H, PW), BF16), DMA((7,)),
         rows, rows, pltpu.VMEM((QR, BLK), F32), gammas, dzp_buf, bz_buf, DMA((CHUNKS + 5,))],
        56, flops=3_000_000_000, nbytes=30_000_000,
    )(codes, queries.T, pair_weight.T, point_weight.reshape(1, H), frame_table, index, cotangent, out_weight, tiles)

    mine, logit, da, stat = call(
        logit_kernel, "logit", [SMEM] + [HBM] * 6, [far((32, QR), F32), far(planes, F32), far(planes, F32), far((N_COL, 32, QR), F32)],
        [pltpu.VMEM((CAP, BLK, 2 * FG), BF16), half, half, marks, gammas, pltpu.VMEM((32, QR), F32), bz_buf, plane_buf,
         plane_buf, DMA((10,)), DMA((H,))], 56,
    )(codes, key_all, qf, df, e, gam, bz)

    stat_all = lax.all_to_all(stat, "col", split_axis=0, concat_axis=0)

    (out,) = call(
        out_kernel, "local_out", [SMEM] + [HBM] * 5, [far((QR, 2048), BF16)],
        [held, pltpu.VMEM((H, BLK, BLK), F32), pltpu.VMEM((H, BLK, PW), F32), pltpu.VMEM((BLK, HJ), BF16),
         pltpu.VMEM((HJ, GF), BF16), sems, plane_buf, half, pltpu.VMEM((32, QR), F32), marks,
         pltpu.VMEM((QR, 2048), F32), pltpu.VMEM((QR, 2048), BF16), DMA((6,))], 56, flops=2_000_000_000, nbytes=20_000_000,
    )(codes, tiles, logit, key_all, mine, e)

    whole, keep, kg, send = call(
        back_kernel, "back", [SMEM] + [HBM] * 10,
        [far((QR, BLK), F32), far((4, OWN, 2560), BF16), far((KR, 2 * FG), BF16), far((4, OWN, 2560), BF16)],
        [pltpu.VMEM((32, QR), F32), pltpu.VMEM((N_COL, 32, QR), F32), half, half, half, marks, gammas, plane_buf, plane_buf,
         pltpu.VMEM((QR, 2048), BF16), DMA((21,)),
         pltpu.VMEM((QR, BLK), F32), pltpu.VMEM((4, OWN, 2560), BF16), pltpu.VMEM((KR, 2 * FG), BF16),
         pltpu.VMEM((4, OWN, 2560), BF16), DMA((4,)),
         pltpu.VMEM((KR, 2 * FG), F32), pltpu.VMEM((BLK, HJ), BF16), pltpu.VMEM((HJ, BLK), BF16),
         pltpu.VMEM((HJ, BLK), BF16), pltpu.VMEM((HJ, GF), BF16), pltpu.VMEM((HJ, GF), BF16),
         pltpu.VMEM((HJ, GF), BF16), pltpu.VMEM((HJ, GF), BF16), pltpu.VMEM((QR, FG), F32),
         pltpu.VMEM((QR, 2560), BF16)], 56,
    )(codes, mine, stat_all, key_all, qf, df, e, gam, logit, da, out)

    kg_all = lax.all_to_all(kg.reshape(N_ROW, OWN, 2 * FG), "row", split_axis=0, concat_axis=0)
    got = lax.ppermute(send, "col", [(d, d ^ 1) for d in range(N_COL)])
    own, *away = call(
        fold_kernel, "fold", [FULL] * 2, [near((OWN, 2560), BF16)] + [free((OWN, 2560), BF16)] * 3, [], 4
    )(keep, got)
    came = [
        lax.ppermute(part, "col", [(d, (d + 2 * k) % N_COL) for d in range(N_COL)])
        for k, part in enumerate(away, 1)
    ]

    (grad_tiles,) = call(
        pair_out_kernel, "pair_out", [SMEM] + [HBM] * 4, [far((CAP * BLK, BLK, PW), BF16)],
        [held, pltpu.VMEM((2 * H, BLK, BLK), F32), sems, plane_buf, plane_buf, dzp_buf,
         pltpu.VMEM((QR, BLK), F32), DMA((2 * CAP + 2,))], 56, flops=4_000_000_000, nbytes=30_000_000,
    )(codes, whole, logit, da, dzp)

    update, grad_queries, grad_keys = call(
        final_kernel, "final", [FULL] * 7 + [HBM],
        [free((OWN, SW), BF16), free((OWN, F), BF16), free((OWN, 2 * F), BF16)],
        [pltpu.VMEM((2016, SW), BF16), DMA((1,))], 12,
    )(kg_all, own, *came, frame_q, frame_k, out_weight)
    return update, grad_queries, grad_keys, grad_tiles.reshape(pair.shape)


def solution(mesh):
    in_specs = (
        P("row", None),
        P(("col", "row"), None),
        P(),
        P(),
        P("row", "col", None),
        P("row", "col", None, None, None, None),
        P(),
        P(),
        P(),
        P("row", None),
    )
    out_specs = (
        P(("row", "col"), None),
        P(("row", "col"), None),
        P(("col", "row"), None),
        P("row", "col", None, None, None, None),
    )
    return jax.shard_map(on_device, mesh=mesh, in_specs=in_specs, out_specs=out_specs, check_vma=False)
```
